128 devices in a mesh: seq: 32 (over x_lo, y, z), res: 4 (over x_hi, core).
Axes of the slice: x: 4 (x_hi: 2, x_lo: 2; x = x_hi * 2 + x_lo), y: 4, z: 4, core: 2. Of those that a mesh axis runs over, the one named last changes fastest.
Arguments:
- alignment_embedding: bfloat16 [256, 512, 768], P('seq', 'res'), may hold values from -6 to 6
- horizontal_scale_vector: float32 [768], replicated, may hold values from 0.1 to 1.9
- horizontal_probe_matrix: bfloat16 [768, 768], replicated, may hold values from -0.21875 to 0.21875
- horizontal_lookup_matrix: bfloat16 [768, 768], replicated, may hold values from -0.21875 to 0.21875
- horizontal_content_matrix: bfloat16 [768, 768], replicated, may hold values from -0.21875 to 0.21875
- horizontal_emit_matrix: bfloat16 [768, 768], replicated, may hold values from -0.21875 to 0.21875
- vertical_scale_vector: float32 [768], replicated, may hold values from 0.1 to 1.9
- vertical_probe_matrix: bfloat16 [768, 768], replicated, may hold values from -0.21875 to 0.21875
- vertical_lookup_matrix: bfloat16 [768, 768], replicated, may hold values from -0.21875 to 0.21875
- vertical_content_matrix: bfloat16 [768, 768], replicated, may hold values from -0.21875 to 0.21875
- vertical_emit_matrix: bfloat16 [768, 768], replicated, may hold values from -0.21875 to 0.21875
Outputs:
- layer_out: bfloat16 [256, 512, 768], P('seq', 'res')
The draws below stay inside these ranges and needn't reach their ends.
All inputs are finite; a program needn't handle non-finite values.
Results may differ from the reference program's by a relative error of at most 0.02.
Values may be sent and summed in bfloat16 or wider, within the bound.
No kernel may reach another device: no remote copies, remote signals or barrier semaphores. Data moves between devices by JAX's collectives and lax.ppermute only.
A program may use at most 128 MiB of HBM per device.

```python
import math
import jax
import jax.numpy as jnp
from jax import lax

HEADS = 12
EMBED_SIZE = 768
ALIGNED_NUMBER = 256
POSITION_NUMBER = 512


def shard_levels(rng, dims, split, low, top_value):
    loudness = 1.0
    for position, blocks in split:
        draws = jax.random.uniform(jax.random.fold_in(jax.random.fold_in(rng, 6), position), (blocks,), jnp.float32, low / len(split), top_value / len(split))
        loudness = loudness * jnp.repeat(jnp.exp(draws), dims[position] // blocks).reshape((-1,) + (1,) * (len(dims) - 1 - position))
    return loudness


def noise(own_key, shape, spread, limit, cuts=(), held_as=jnp.bfloat16):
    factor_of = shard_levels(own_key, shape, cuts, -0.22, 0.18) if cuts else 1.0
    values = jax.random.normal(own_key, shape, jnp.float32) * spread * factor_of
    return jnp.minimum(jnp.maximum(values, -limit), limit).astype(held_as)


def setup_inputs(seed: int = 0) -> dict:
    keys = jax.random.split(jax.random.key(seed), 12)
    return {
        "alignment_embedding": noise(keys[0], (ALIGNED_NUMBER, POSITION_NUMBER, EMBED_SIZE), 1.0, 6.0, ((0, 32), (1, 4))),
        "horizontal_scale_vector": jnp.clip(1.0 + 0.18 * jax.random.normal(keys[1], (EMBED_SIZE,), jnp.float32), 0.1, 1.9),
        "horizontal_probe_matrix": noise(keys[2], (EMBED_SIZE, EMBED_SIZE), EMBED_SIZE ** -0.5, 0.21875),
        "horizontal_lookup_matrix": noise(keys[3], (EMBED_SIZE, EMBED_SIZE), EMBED_SIZE ** -0.5, 0.21875),
        "horizontal_content_matrix": noise(keys[4], (EMBED_SIZE, EMBED_SIZE), EMBED_SIZE ** -0.5, 0.21875),
        "horizontal_emit_matrix": noise(keys[5], (EMBED_SIZE, EMBED_SIZE), EMBED_SIZE ** -0.5, 0.21875),
        "vertical_scale_vector": jnp.clip(1.0 + 0.18 * jax.random.normal(keys[6], (EMBED_SIZE,), jnp.float32), 0.1, 1.9),
        "vertical_probe_matrix": noise(keys[7], (EMBED_SIZE, EMBED_SIZE), EMBED_SIZE ** -0.5, 0.21875),
        "vertical_lookup_matrix": noise(keys[8], (EMBED_SIZE, EMBED_SIZE), EMBED_SIZE ** -0.5, 0.21875),
        "vertical_content_matrix": noise(keys[9], (EMBED_SIZE, EMBED_SIZE), EMBED_SIZE ** -0.5, 0.21875),
        "vertical_emit_matrix": noise(keys[10], (EMBED_SIZE, EMBED_SIZE), EMBED_SIZE ** -0.5, 0.21875),
    }


def standardize_features(inputs, gain_vec):
    values32 = inputs.astype(jnp.float32)
    average = lax.optimization_barrier(jnp.mean(values32, axis=-1, keepdims=True))
    centered = values32 - average
    variance = lax.optimization_barrier(jnp.mean(centered * centered, axis=-1, keepdims=True))
    return (centered * lax.rsqrt(variance + 1e-05) * gain_vec).astype(jnp.bfloat16)

def project(inputs, matrix):
    flat_rows = inputs.reshape(-1, inputs.shape[-1])
    result = jnp.dot(flat_rows, matrix, preferred_element_type=jnp.float32).astype(jnp.bfloat16)
    return result.reshape(inputs.shape[:-1] + (matrix.shape[1],))

def attend_columns(queries, keys_in, values_in):
    alignment_span_full, count, feature_breadth = queries.shape
    head_dim = feature_breadth // HEADS
    q_four = queries.astype(jnp.float32).reshape(alignment_span_full, count, HEADS, head_dim)
    k_four = keys_in.astype(jnp.float32).reshape(alignment_span_full, count, HEADS, head_dim)
    v_four = values_in.astype(jnp.float32).reshape(alignment_span_full, count, HEADS, head_dim)
    logits = jnp.einsum('anhd,bnhd->nhab', q_four, k_four) * (1.0 / math.sqrt(head_dim))
    weights_col = jax.nn.softmax(logits, axis=-1).astype(jnp.bfloat16)
    result = jnp.einsum('nhab,bnhd->anhd', weights_col.astype(jnp.float32), v_four)
    return result.astype(jnp.bfloat16).reshape(alignment_span_full, count, feature_breadth)

def reference(alignment_embedding, horizontal_scale_vector, horizontal_probe_matrix, horizontal_lookup_matrix, horizontal_content_matrix, horizontal_emit_matrix, vertical_scale_vector, vertical_probe_matrix, vertical_lookup_matrix, vertical_content_matrix, vertical_emit_matrix):
    alignment_span_full, position_span_full, feature_breadth = alignment_embedding.shape
    head_dim = feature_breadth // HEADS
    standardized_embedding = standardize_features(alignment_embedding, horizontal_scale_vector)
    q_four = project(standardized_embedding, horizontal_probe_matrix).astype(jnp.float32).reshape(alignment_span_full, position_span_full, HEADS, head_dim)
    k_four = project(standardized_embedding, horizontal_lookup_matrix).astype(jnp.float32).reshape(alignment_span_full, position_span_full, HEADS, head_dim)
    v_four = project(standardized_embedding, horizontal_content_matrix).astype(jnp.float32).reshape(alignment_span_full, position_span_full, HEADS, head_dim)
    scaling = 1.0 / (math.sqrt(head_dim) * math.sqrt(alignment_span_full))
    tied = jnp.einsum('rihd,rjhd->hij', q_four, k_four) * scaling
    weights_row = jax.nn.softmax(tied, axis=-1).astype(jnp.bfloat16)
    horizontal_mixing_result = jnp.einsum('hij,rjhd->rihd', weights_row.astype(jnp.float32), v_four)
    horizontal_mixing_result = horizontal_mixing_result.astype(jnp.bfloat16).reshape(alignment_span_full * position_span_full, feature_breadth)
    running_embedding = alignment_embedding.astype(jnp.float32) + jnp.dot(horizontal_mixing_result, horizontal_emit_matrix, preferred_element_type=jnp.float32).reshape(alignment_span_full, position_span_full, feature_breadth)
    running_embedding = running_embedding.astype(jnp.bfloat16)
    normed_col = standardize_features(running_embedding, vertical_scale_vector)
    block_cols = 16
    block_count = position_span_full // block_cols

    def one_block(block_idx):
        start = (block_idx * block_cols).astype(jnp.int32)
        piece = lax.dynamic_slice_in_dim(normed_col, start, block_cols, 1)
        return attend_columns(project(piece, vertical_probe_matrix), project(piece, vertical_lookup_matrix), project(piece, vertical_content_matrix))
    stacked = lax.map(one_block, jnp.arange(block_count, dtype=jnp.int32))
    col_mix = jnp.transpose(stacked, (1, 0, 2, 3)).reshape(alignment_span_full * position_span_full, feature_breadth)
    layer_out = running_embedding.astype(jnp.float32) + jnp.dot(col_mix, vertical_emit_matrix, preferred_element_type=jnp.float32).reshape(alignment_span_full, position_span_full, feature_breadth)
    return layer_out.astype(jnp.bfloat16)
```

```python
import math

import jax
import jax.numpy as jnp
from jax import lax
from jax.sharding import PartitionSpec as P

HEADS = 12
SEQ = 32
CORE_SWAP = [(0, 1), (1, 0), (2, 3), (3, 2)]
XHI_SWAP = [(0, 2), (1, 3), (2, 0), (3, 1)]


def norm(x, gain):
    v = x.astype(jnp.float32)
    c = v - jnp.mean(v, axis=-1, keepdims=True)
    var = jnp.mean(c * c, axis=-1, keepdims=True)
    return (c * lax.rsqrt(var + 1e-05) * gain).astype(jnp.bfloat16)


def project(x, w):
    r = jnp.dot(x.reshape(-1, x.shape[-1]), w, preferred_element_type=jnp.float32).astype(jnp.bfloat16)
    return r.reshape(x.shape[:-1] + (w.shape[1],))


def heads(x):
    return x.reshape(x.shape[:-1] + (HEADS, x.shape[-1] // HEADS))


def a2a(x):
    return lax.all_to_all(x, "seq", split_axis=0, concat_axis=0, tiled=True)


def shards(x, hg, wq, wk, wv, wo, vg, cq, ck, cv, co):
    S, N, F = x.shape
    D = F // HEADS
    n0 = norm(x, hg)
    sib = lax.ppermute(n0, "res", CORE_SWAP)
    xh = lax.ppermute(n0, "res", XHI_SWAP)
    xhs = lax.ppermute(xh, "res", CORE_SWAP)
    q = project(n0, wq)

    def logits(a, b):
        k = jnp.concatenate([project(a, wk), project(b, wk)], axis=1)
        l = jnp.einsum("sihd,sjhd->hij", heads(q), heads(k), preferred_element_type=jnp.float32)
        l = l.astype(jnp.bfloat16).reshape(SEQ, HEADS * N // SEQ, 2 * N)
        return jnp.sum(a2a(l).astype(jnp.float32), axis=0)

    scale = 1.0 / (math.sqrt(D) * math.sqrt(S * SEQ))
    tied = jnp.concatenate([logits(n0, sib), logits(xh, xhs)], axis=-1) * scale
    probs = jax.nn.softmax(tied, axis=-1).astype(jnp.bfloat16)
    probs = a2a(jnp.broadcast_to(probs[None], (SEQ,) + probs.shape)).reshape(HEADS, N, 4 * N)
    v = jnp.concatenate([project(t, wv) for t in (n0, sib, xh, xhs)], axis=1)
    mix = jnp.einsum("hij,sjhd->sihd", probs, heads(v), preferred_element_type=jnp.float32)
    mix = mix.astype(jnp.bfloat16).reshape(S * N, F)
    hid = x.astype(jnp.float32) + jnp.dot(mix, wo, preferred_element_type=jnp.float32).reshape(x.shape)
    hid = hid.astype(jnp.bfloat16)
    G = N // SEQ
    t = jnp.transpose(hid.reshape(S, SEQ, G, F), (1, 2, 0, 3))
    t = a2a(t)
    hc = jnp.transpose(t, (1, 0, 2, 3)).reshape(G, SEQ * S, F)
    nc = norm(hc, vg)
    q, k, v = (heads(project(nc, w)) for w in (cq, ck, cv))
    l = jnp.einsum("nahd,nbhd->nhab", q, k, preferred_element_type=jnp.float32) * (1.0 / math.sqrt(D))
    w = jax.nn.softmax(l, axis=-1).astype(jnp.bfloat16)
    m = jnp.einsum("nhab,nbhd->nahd", w, v, preferred_element_type=jnp.float32).astype(jnp.bfloat16)
    o = hc.astype(jnp.float32) + jnp.dot(
        m.reshape(-1, F), co, preferred_element_type=jnp.float32
    ).reshape(hc.shape)
    o = o.astype(jnp.bfloat16).reshape(G, SEQ, S, F)
    o = a2a(jnp.transpose(o, (1, 0, 2, 3)))
    return jnp.transpose(o, (2, 0, 1, 3)).reshape(S, N, F)


def solution(mesh):
    in_specs = (P("seq", "res", None),) + (P(),) * 10
    return jax.shard_map(shards, mesh=mesh, in_specs=in_specs, out_specs=P("seq", "res", None), check_vma=False)
```

```python
import functools
import math

import jax
import jax.numpy as jnp
from jax import lax
from jax.experimental import pallas as pl
from jax.experimental.pallas import tpu as pltpu
from jax.sharding import PartitionSpec as P

HEADS = 12
D = 64
SEQ = 32
CORE_SWAP = [(0, 1), (1, 0), (2, 3), (3, 2)]
XHI_SWAP = [(0, 2), (1, 3), (2, 0), (3, 1)]
F32 = jnp.float32
BF16 = jnp.bfloat16
PARAMS = pltpu.CompilerParams(vmem_limit_bytes=56 * 1024 * 1024)


def norm(x, gain):
    v = x.astype(F32)
    c = v - jnp.mean(v, axis=-1, keepdims=True)
    var = jnp.mean(c * c, axis=-1, keepdims=True)
    return (c * lax.rsqrt(var + 1e-05) * gain).astype(BF16)


def mm(a, b):
    return lax.dot_general(a, b, (((1,), (0,)), ((), ())), preferred_element_type=F32)


def mm_t(a, b):
    return lax.dot_general(a, b, (((1,), (1,)), ((), ())), preferred_element_type=F32)


def head(x, h):
    return x[:, h * D : (h + 1) * D]


def pair_store(ref, y0, y1, lane):
    for h in range(HEADS):
        ref[h, :, pl.ds(lane, 2 * D)] = jnp.concatenate([head(y0, h), head(y1, h)], axis=1)


def whole(shape):
    return pl.BlockSpec(shape, lambda *_: (0,) * len(shape))


def logits_kernel(first, *refs):
    if first:
        xa, xb, g, wk, wq, q, out, ks = refs
    else:
        xa, xb, g, wk, q, out, ks = refs
    t = pl.program_id(0)
    n = xa.shape[1]
    lane = pl.multiple_of(t * 2 * D, 2 * D)
    f = xa.shape[2]
    na = norm(xa[...].reshape(2 * n, f), g[...])
    nb = norm(xb[...].reshape(2 * n, f), g[...])
    ka = mm(na, wk[...]).astype(BF16)
    kb = mm(nb, wk[...]).astype(BF16)
    for h in range(HEADS):
        ks[h, 0:n, pl.ds(lane, 2 * D)] = jnp.concatenate([head(ka[:n], h), head(ka[n:], h)], axis=1)
        ks[h, n : 2 * n, pl.ds(lane, 2 * D)] = jnp.concatenate([head(kb[:n], h), head(kb[n:], h)], axis=1)
    if first:
        qq = mm(na, wq[...]).astype(BF16)
        pair_store(q, qq[:n], qq[n:], lane)

    @pl.when(t == pl.num_programs(0) - 1)
    def _():
        for h in range(HEADS):
            out[h] = mm_t(q[h], ks[h]).astype(BF16)


def logits(xa, xb, g, wk, wq=None, q=None):
    s, n, f = xa.shape
    first = q is None
    xs = pl.BlockSpec((2, n, f), lambda t: (t, 0, 0))
    in_specs = [xs, xs, whole(g.shape), whole(wk.shape)]
    qshape = (HEADS, n, s * D)
    lshape = (HEADS, n, 2 * n)
    in_specs += [whole(wq.shape)] if first else [whole(qshape)]
    ospecs = [whole(qshape), whole(lshape)] if first else [whole(lshape)]
    oshape = [jax.ShapeDtypeStruct(qshape, BF16), jax.ShapeDtypeStruct(lshape, BF16)]
    return pl.pallas_call(
        functools.partial(logits_kernel, first),
        grid=(s // 2,),
        in_specs=in_specs,
        out_specs=ospecs,
        out_shape=oshape if first else oshape[1:],
        scratch_shapes=[pltpu.VMEM((HEADS, 2 * n, s * D), BF16)],
        compiler_params=PARAMS,
        name="logits",
    )(xa, xb, g, wk, wq if first else q)


def values_kernel(xa, xb, g, wv, out):
    n, f = xa.shape[1], xa.shape[2]
    va = mm(norm(xa[...].reshape(2 * n, f), g[...]), wv[...]).astype(BF16)
    vb = mm(norm(xb[...].reshape(2 * n, f), g[...]), wv[...]).astype(BF16)
    for h in range(HEADS):
        out[h, 0:n] = jnp.concatenate([head(va[:n], h), head(va[n:], h)], axis=1)
        out[h, n : 2 * n] = jnp.concatenate([head(vb[:n], h), head(vb[n:], h)], axis=1)


def values(xa, xb, g, wv):
    s, n, f = xa.shape
    xs = pl.BlockSpec((2, n, f), lambda t: (t, 0, 0))
    return pl.pallas_call(
        values_kernel,
        grid=(s // 2,),
        in_specs=[xs, xs, whole(g.shape), whole(wv.shape)],
        out_specs=pl.BlockSpec((HEADS, 2 * n, 2 * D), lambda t: (0, 0, t)),
        out_shape=jax.ShapeDtypeStruct((HEADS, 2 * n, s * D), BF16),
        compiler_params=PARAMS,
        name="values",
    )(xa, xb, g, wv)


def mix_kernel(p, v1, v2, x, wo, out, ms):
    t = pl.program_id(0)
    n = p.shape[1]
    s = x.shape[0]
    lane = pl.multiple_of(t * 2 * D, 2 * D)
    o = []
    for h in range(2):
        o.append((mm(p[h, :, : 2 * n], v1[h]) + mm(p[h, :, 2 * n :], v2[h])).astype(BF16))
    for r in range(s):
        ms[r, :, pl.ds(lane, 2 * D)] = jnp.concatenate([head(o[0], r), head(o[1], r)], axis=1)

    @pl.when(t == pl.num_programs(0) - 1)
    def _():
        for r in range(s):
            out[r] = (x[r].astype(F32) + mm(ms[r], wo[...])).astype(BF16)


def mix(p, v1, v2, x, wo):
    s, n, f = x.shape
    vs = pl.BlockSpec((2, 2 * n, s * D), lambda t: (t, 0, 0))
    return pl.pallas_call(
        mix_kernel,
        grid=(HEADS // 2,),
        in_specs=[pl.BlockSpec((2, n, 4 * n), lambda t: (t, 0, 0)), vs, vs, whole(x.shape), whole(wo.shape)],
        out_specs=whole(x.shape),
        out_shape=jax.ShapeDtypeStruct(x.shape, BF16),
        scratch_shapes=[pltpu.VMEM((s, n, f), BF16)],
        compiler_params=PARAMS,
        name="mix",
    )(p, v1, v2, x, wo)


def column_kernel(h_ref, g, wq, wk, wv, wo, out, ms):
    x = h_ref[0].astype(F32)
    n = norm(x, g[...])
    q = (mm(n, wq[...]) * (1.0 / (math.sqrt(D) * math.log(2.0)))).astype(BF16)
    k = mm(n, wk[...]).astype(BF16)
    v = mm(n, wv[...]).astype(BF16)
    for hp in range(HEADS // 2):
        pair = []
        for h in (2 * hp, 2 * hp + 1):
            l = mm_t(head(q, h), head(k, h))
            e = jnp.exp2(l - jnp.max(l, axis=-1, keepdims=True))
            d = jnp.sum(e, axis=-1, keepdims=True)
            pair.append((mm(e.astype(BF16), head(v, h)) / d).astype(BF16))
        ms[:, hp * 2 * D : (hp + 1) * 2 * D] = jnp.concatenate(pair, axis=1)
    out[0] = (x + mm(ms[...], wo[...])).astype(BF16)


def column(hc, g, wq, wk, wv, wo):
    c, a, f = hc.shape
    xs = pl.BlockSpec((1, a, f), lambda t: (t, 0, 0))
    return pl.pallas_call(
        column_kernel,
        grid=(c,),
        in_specs=[xs, whole(g.shape)] + [whole(w.shape) for w in (wq, wk, wv, wo)],
        out_specs=xs,
        out_shape=jax.ShapeDtypeStruct(hc.shape, BF16),
        scratch_shapes=[pltpu.VMEM((a, f), BF16)],
        compiler_params=PARAMS,
        name="column",
    )(hc, g, wq, wk, wv, wo)


def a2a(x):
    return lax.all_to_all(x, "seq", split_axis=0, concat_axis=0, tiled=True)


def shards(x, hg, wq, wk, wv, wo, vg, cq, ck, cv, co):
    S, N, F = x.shape
    hg = hg.reshape(1, F)
    vg = vg.reshape(1, F)
    xh = lax.ppermute(x, "res", XHI_SWAP)
    sib = lax.ppermute(x, "res", CORE_SWAP)
    xhs = lax.ppermute(xh, "res", CORE_SWAP)

    def reduce(l):
        return jnp.sum(a2a(l.reshape(SEQ, HEADS * N // SEQ, 2 * N)).astype(F32), axis=0)

    q, l1 = logits(x, sib, hg, wk, wq=wq)
    r1 = reduce(l1)
    v1 = values(x, sib, hg, wv)
    (l2,) = logits(xh, xhs, hg, wk, q=q)
    r2 = reduce(l2)
    v2 = values(xh, xhs, hg, wv)
    scale = 1.0 / (math.sqrt(D) * math.sqrt(S * SEQ))
    probs = jax.nn.softmax(jnp.concatenate([r1, r2], axis=-1) * scale, axis=-1).astype(BF16)
    probs = a2a(jnp.broadcast_to(probs[None], (SEQ,) + probs.shape)).reshape(HEADS, N, 4 * N)
    hid = mix(probs, v1, v2, x, wo)
    G = N // SEQ
    t = a2a(jnp.transpose(hid.reshape(S, SEQ, G, F), (1, 2, 0, 3)))
    hc = jnp.transpose(t, (1, 0, 2, 3)).reshape(G, SEQ * S, F)
    o = column(hc, vg, cq, ck, cv, co).reshape(G, SEQ, S, F)
    o = a2a(jnp.transpose(o, (1, 0, 2, 3)))
    return jnp.transpose(o, (2, 0, 1, 3)).reshape(S, N, F)


def solution(mesh):
    in_specs = (P("seq", "res", None),) + (P(),) * 10
    return jax.shard_map(shards, mesh=mesh, in_specs=in_specs, out_specs=P("seq", "res", None), check_vma=False)
```

```python
import functools
import math

import jax
import jax.numpy as jnp
from jax import lax
from jax.experimental import pallas as pl
from jax.experimental.pallas import tpu as pltpu
from jax.sharding import PartitionSpec as P

HEADS = 12
D = 64
SEQ = 32
CORE_SWAP = [(0, 1), (1, 0), (2, 3), (3, 2)]
XHI_SWAP = [(0, 2), (1, 3), (2, 0), (3, 1)]
F32 = jnp.float32
BF16 = jnp.bfloat16
PARAMS = pltpu.CompilerParams(vmem_limit_bytes=56 * 1024 * 1024)


def norm(x, gain):
    v = x.astype(F32)
    c = v - jnp.mean(v, axis=-1, keepdims=True)
    var = jnp.mean(c * c, axis=-1, keepdims=True)
    return (c * lax.rsqrt(var + 1e-05) * gain).astype(BF16)


def mm(a, b):
    return lax.dot_general(a, b, (((1,), (0,)), ((), ())), preferred_element_type=F32)


def mm_t(a, b):
    return lax.dot_general(a, b, (((1,), (1,)), ((), ())), preferred_element_type=F32)


def head(x, h):
    return x[:, h * D : (h + 1) * D]


def whole(shape):
    return pl.BlockSpec(shape, lambda *_: (0,) * len(shape))


def pair(y, n, h):
    return jnp.concatenate([head(y[:n], h), head(y[n:], h)], axis=1)


def logits_kernel(first, *refs):
    if first:
        xa, xb, g, wk, wq, q, out, ks = refs
    else:
        xa, xb, g, wk, q, out, ks = refs
    t = pl.program_id(0)
    n, f = xa.shape[1:]
    lane = pl.multiple_of(t * 2 * D, 2 * D)
    na = norm(xa[...].reshape(2 * n, f), g[...])
    nb = norm(xb[...].reshape(2 * n, f), g[...])
    ka = mm(na, wk[...]).astype(BF16)
    kb = mm(nb, wk[...]).astype(BF16)
    for h in range(HEADS):
        ks[h, 0:n, pl.ds(lane, 2 * D)] = pair(ka, n, h)
        ks[h, n : 2 * n, pl.ds(lane, 2 * D)] = pair(kb, n, h)
    if first:
        qq = mm(na, wq[...]).astype(BF16)
        for h in range(HEADS):
            q[h, :, pl.ds(lane, 2 * D)] = pair(qq, n, h)

    @pl.when(t == pl.num_programs(0) - 1)
    def _():
        for h in range(HEADS):
            out[h] = mm_t(q[h], ks[h]).astype(BF16)


def logits(xa, xb, g, wk, wq=None, q=None):
    s, n, f = xa.shape
    first = q is None
    m = n if first else q.shape[1]
    xs = pl.BlockSpec((2, n, f), lambda t: (t, 0, 0))
    in_specs = [xs, xs, whole(g.shape), whole(wk.shape)]
    qshape = (HEADS, m, s * D)
    lshape = (HEADS, m, 2 * n)
    in_specs += [whole(wq.shape)] if first else [whole(qshape)]
    ospecs = [whole(qshape), whole(lshape)] if first else [whole(lshape)]
    oshape = [jax.ShapeDtypeStruct(qshape, BF16), jax.ShapeDtypeStruct(lshape, BF16)]
    return pl.pallas_call(
        functools.partial(logits_kernel, first),
        grid=(s // 2,),
        in_specs=in_specs,
        out_specs=ospecs,
        out_shape=oshape if first else oshape[1:],
        scratch_shapes=[pltpu.VMEM((HEADS, 2 * n, s * D), BF16)],
        compiler_params=PARAMS,
        name="logits",
    )(xa, xb, g, wk, wq if first else q)


def values_kernel(*refs):
    xs, (g, wv, out) = refs[:-3], refs[-3:]
    at = 0
    for x in xs:
        n, f = x.shape[1:]
        v = mm(norm(x[...].reshape(2 * n, f), g[...]), wv[...]).astype(BF16)
        for h in range(HEADS):
            out[h, at : at + n] = pair(v, n, h)
        at += n


def values(pieces, g, wv):
    s, _, f = pieces[0].shape
    total = sum(p.shape[1] for p in pieces)
    specs = [pl.BlockSpec((2, p.shape[1], f), lambda t: (t, 0, 0)) for p in pieces]
    return pl.pallas_call(
        values_kernel,
        grid=(s // 2,),
        in_specs=specs + [whole(g.shape), whole(wv.shape)],
        out_specs=pl.BlockSpec((HEADS, total, 2 * D), lambda t: (0, 0, t)),
        out_shape=jax.ShapeDtypeStruct((HEADS, total, s * D), BF16),
        compiler_params=PARAMS,
        name="values",
    )(*pieces, g, wv)


def mix_kernel(p, v, x, wo, out, ms):
    t = pl.program_id(0)
    s = x.shape[0]
    lane = pl.multiple_of(t * 2 * D, 2 * D)
    o = [mm(p[h], v[h]).astype(BF16) for h in range(2)]
    for r in range(s):
        ms[r, :, pl.ds(lane, 2 * D)] = jnp.concatenate([head(o[0], r), head(o[1], r)], axis=1)

    @pl.when(t == pl.num_programs(0) - 1)
    def _():
        for r in range(s):
            out[r] = (x[r].astype(F32) + mm(ms[r], wo[...])).astype(BF16)


def mix(p, v, x, wo):
    s, n, f = x.shape
    return pl.pallas_call(
        mix_kernel,
        grid=(HEADS // 2,),
        in_specs=[
            pl.BlockSpec((2,) + p.shape[1:], lambda t: (t, 0, 0)),
            pl.BlockSpec((2,) + v.shape[1:], lambda t: (t, 0, 0)),
            whole(x.shape),
            whole(wo.shape),
        ],
        out_specs=whole(x.shape),
        out_shape=jax.ShapeDtypeStruct(x.shape, BF16),
        scratch_shapes=[pltpu.VMEM((s, n, f), BF16)],
        compiler_params=PARAMS,
        name="mix",
    )(p, v, x, wo)


def column_kernel(h_ref, g, wq, wk, wv, wo, out, xs, ns, qs, ks, vs, ms):
    src, rows, f = h_ref.shape
    a = src * 8
    for i in range(0, rows, 16):
        y = h_ref[:, i : i + 16].astype(F32)
        for j in range(2):
            xs[pl.ds((i // 8 + j) * a, a)] = y[:, 8 * j : 8 * j + 8].reshape(a, f)

    def project(p, carry):
        r = pl.ds(pl.multiple_of(p * a, a), a)
        n = norm(xs[r], g[...])
        qs[r] = (mm(n, wq[...]) * (1.0 / (math.sqrt(D) * math.log(2.0)))).astype(BF16)
        ks[r] = mm(n, wk[...]).astype(BF16)
        vs[r] = mm(n, wv[...]).astype(BF16)
        return carry

    def attend(p, carry):
        r = pl.ds(pl.multiple_of(p * a, a), a)
        low = lax.broadcasted_iota(jnp.int32, (a, 2 * D), 1) < D
        zero = jnp.zeros((a, 2 * D), BF16)
        ones = jnp.ones((a, 2 * D), BF16)
        for hp in range(HEADS // 2):
            c = slice(hp * 2 * D, (hp + 1) * 2 * D)
            q, k = qs[r, c], ks[r, c]
            v = jnp.concatenate([vs[r, c], ones], axis=1)
            o = []
            for kh in (jnp.where(low, k, zero), jnp.where(low, zero, k)):
                l = mm_t(q, kh)
                e = jnp.exp2(l - jnp.max(l, axis=-1, keepdims=True)).astype(BF16)
                w = mm(e, v)
                o.append(w[:, : 2 * D] / w[:, 2 * D :])
            ms[r, c] = jnp.where(low, o[0], o[1]).astype(BF16)
        return carry

    def emit(p, carry):
        r = pl.ds(pl.multiple_of(p * a, a), a)
        xs[r] = xs[r] + mm(ms[r], wo[...])
        return carry

    lax.fori_loop(0, rows // 8, project, 0)
    lax.fori_loop(0, rows // 8, attend, 0)
    lax.fori_loop(0, rows // 8, emit, 0)
    for i in range(0, rows, 16):
        y = [xs[pl.ds((i // 8 + j) * a, a)].reshape(src, 8, f) for j in range(2)]
        out[:, i : i + 16] = jnp.concatenate(y, axis=1).astype(BF16)


def column(hc, g, wq, wk, wv, wo):
    src, rows, f = hc.shape
    m = src * rows
    return pl.pallas_call(
        column_kernel,
        out_shape=jax.ShapeDtypeStruct(hc.shape, BF16),
        scratch_shapes=[pltpu.VMEM((m, f), F32)] + [pltpu.VMEM((m, f), BF16)] * 5,
        compiler_params=PARAMS,
        name="column",
    )(hc, g, wq, wk, wv, wo)


def a2a(x):
    return lax.all_to_all(x, "seq", split_axis=0, concat_axis=0, tiled=True)


def shards(x, hg, wq, wk, wv, wo, vg, cq, ck, cv, co):
    S, N, F = x.shape
    hg = hg.reshape(1, F)
    vg = vg.reshape(1, F)
    barrier = lax.optimization_barrier

    def reduce(l):
        return a2a(l.reshape(SEQ, HEADS * N // SEQ, l.shape[-1]))

    xh = lax.ppermute(x, "res", XHI_SWAP)
    sib = lax.ppermute(x, "res", CORE_SWAP)
    q, l1 = logits(x, sib, hg, wk, wq=wq)
    r1 = jnp.sum(reduce(l1).astype(F32), axis=0)
    xh, r1 = barrier((xh, r1))
    xhs = lax.ppermute(xh, "res", CORE_SWAP)
    (l2,) = logits(xh, xhs, hg, wk, q=q)
    r2 = jnp.sum(reduce(l2).astype(F32), axis=0)
    x_late, l2 = barrier((x, l2))
    v = values((x_late, sib, xh, xhs), hg, wv)
    scale = 1.0 / (math.sqrt(D) * math.sqrt(S * SEQ))
    tied = jnp.concatenate([r1, r2], axis=-1) * scale
    probs = jax.nn.softmax(tied, axis=-1).astype(BF16)
    probs = a2a(jnp.broadcast_to(probs[None], (SEQ,) + probs.shape)).reshape(HEADS, N, 4 * N)
    hid = mix(probs, v, x, wo)
    G = N // SEQ
    t = jnp.transpose(hid.reshape(S, SEQ, G, F), (1, 2, 0, 3)).reshape(SEQ, G * S, F)
    o = a2a(column(a2a(t), vg, cq, ck, cv, co))
    return jnp.transpose(o.reshape(SEQ, G, S, F), (2, 0, 1, 3)).reshape(S, N, F)


def solution(mesh):
    in_specs = (P("seq", "res", None),) + (P(),) * 10
    return jax.shard_map(shards, mesh=mesh, in_specs=in_specs, out_specs=P("seq", "res", None), check_vma=False)
```

```python
import functools
import math

import jax
import jax.numpy as jnp
from jax import lax
from jax.experimental import pallas as pl
from jax.experimental.pallas import tpu as pltpu
from jax.sharding import PartitionSpec as P

HEADS = 12
D = 64
SEQ = 32
CORE_SWAP = [(0, 1), (1, 0), (2, 3), (3, 2)]
XHI_SWAP = [(0, 2), (1, 3), (2, 0), (3, 1)]
F32 = jnp.float32
BF16 = jnp.bfloat16
PARAMS = pltpu.CompilerParams(vmem_limit_bytes=40 * 1024 * 1024)


def norm(x, gain):
    v = x.astype(F32)
    c = v - jnp.mean(v, axis=-1, keepdims=True)
    var = jnp.mean(c * c, axis=-1, keepdims=True)
    return (c * lax.rsqrt(var + 1e-05) * gain).astype(BF16)


def mm(a, b):
    return lax.dot_general(a, b, (((1,), (0,)), ((), ())), preferred_element_type=F32)


def mm_t(a, b):
    return lax.dot_general(a, b, (((1,), (1,)), ((), ())), preferred_element_type=F32)


def head(x, h):
    return x[:, h * D : (h + 1) * D]


def near(*arrays):
    return [pltpu.with_memory_space_constraint(a, pltpu.VMEM) for a in arrays]


def far(*arrays):
    return [pltpu.with_memory_space_constraint(a, pltpu.HBM) for a in arrays]


def whole(shape):
    return pl.BlockSpec(shape, lambda *_: (0,) * len(shape))


def pair(y, n, h):
    return jnp.concatenate([head(y[:n], h), head(y[n:], h)], axis=1)


def logits_kernel(first, *refs):
    if first:
        xa, xb, g, wk, wq, q, out, ks = refs
    else:
        xa, xb, g, wk, q, out, ks = refs
    t = pl.program_id(0)
    n, f = xa.shape[1:]
    lane = pl.multiple_of(t * 2 * D, 2 * D)
    na = norm(xa[...].reshape(2 * n, f), g[...])
    nb = norm(xb[...].reshape(2 * n, f), g[...])
    ka = mm(na, wk[...]).astype(BF16)
    kb = mm(nb, wk[...]).astype(BF16)
    for h in range(HEADS):
        ks[h, 0:n, pl.ds(lane, 2 * D)] = pair(ka, n, h)
        ks[h, n : 2 * n, pl.ds(lane, 2 * D)] = pair(kb, n, h)
    if first:
        qq = mm(na, wq[...]).astype(BF16)
        for h in range(HEADS):
            q[h, :, pl.ds(lane, 2 * D)] = pair(qq, n, h)

    @pl.when(t == pl.num_programs(0) - 1)
    def _():
        for h in range(HEADS):
            out[h] = mm_t(q[h], ks[h]).astype(BF16)


def logits(xa, xb, g, wk, wq=None, q=None):
    s, n, f = xa.shape
    first = q is None
    m = n if first else q.shape[1]
    xs = pl.BlockSpec((2, n, f), lambda t: (t, 0, 0))
    in_specs = [xs, xs, whole(g.shape), whole(wk.shape)]
    qshape = (HEADS, m, s * D)
    lshape = (HEADS, m, 2 * n)
    in_specs += [whole(wq.shape)] if first else [whole(qshape)]
    ospecs = [whole(qshape), whole(lshape)] if first else [whole(lshape)]
    oshape = [jax.ShapeDtypeStruct(qshape, BF16), jax.ShapeDtypeStruct(lshape, BF16)]
    return pl.pallas_call(
        functools.partial(logits_kernel, first),
        grid=(s // 2,),
        in_specs=in_specs,
        out_specs=ospecs,
        out_shape=oshape if first else oshape[1:],
        scratch_shapes=[pltpu.VMEM((HEADS, 2 * n, s * D), BF16)],
        compiler_params=PARAMS,
        name="logits",
    )(*(far(xa, xb) if first else near(xa, xb)), *far(g, wk, wq if first else q))


def values_kernel(*refs):
    xs, (g, wv, out) = refs[:-3], refs[-3:]
    at = 0
    for x in xs:
        n, f = x.shape[1:]
        v = mm(norm(x[...].reshape(2 * n, f), g[...]), wv[...]).astype(BF16)
        for h in range(HEADS):
            out[h, at : at + n] = pair(v, n, h)
        at += n


def values(pieces, g, wv):
    s, _, f = pieces[0].shape
    total = sum(p.shape[1] for p in pieces)
    specs = [pl.BlockSpec((2, p.shape[1], f), lambda t: (t, 0, 0)) for p in pieces]
    return pl.pallas_call(
        values_kernel,
        grid=(s // 2,),
        in_specs=specs + [whole(g.shape), whole(wv.shape)],
        out_specs=pl.BlockSpec((HEADS, total, 2 * D), lambda t: (0, 0, t)),
        out_shape=jax.ShapeDtypeStruct((HEADS, total, s * D), BF16),
        compiler_params=PARAMS,
        name="values",
    )(*far(*pieces, g, wv))


def mix_kernel(p, v, x, wo, out, ms):
    t = pl.program_id(0)
    s = x.shape[0]
    lane = pl.multiple_of(t * 2 * D, 2 * D)
    o = [mm(p[h], v[h]).astype(BF16) for h in range(2)]
    for r in range(s):
        ms[r, :, pl.ds(lane, 2 * D)] = jnp.concatenate([head(o[0], r), head(o[1], r)], axis=1)

    @pl.when(t == pl.num_programs(0) - 1)
    def _():
        for r in range(s):
            out[r] = (x[r].astype(F32) + mm(ms[r], wo[...])).astype(BF16)


def mix(p, v, x, wo):
    s, n, f = x.shape
    return pl.pallas_call(
        mix_kernel,
        grid=(HEADS // 2,),
        in_specs=[
            pl.BlockSpec((2,) + p.shape[1:], lambda t: (t, 0, 0)),
            pl.BlockSpec((2,) + v.shape[1:], lambda t: (t, 0, 0)),
            whole(x.shape),
            whole(wo.shape),
        ],
        out_specs=whole(x.shape),
        out_shape=jax.ShapeDtypeStruct(x.shape, BF16),
        scratch_shapes=[pltpu.VMEM((s, n, f), BF16)],
        compiler_params=PARAMS,
        name="mix",
    )(*near(p), *far(v, x, wo))


def column_kernel(h_ref, g, wq, wk, wv, wo, out, xs, ns, qs, ks, vs, ms):
    src, rows, f = h_ref.shape
    a = src * 8
    for i in range(0, rows, 16):
        y = h_ref[:, i : i + 16].astype(F32)
        for j in range(2):
            xs[pl.ds((i // 8 + j) * a, a)] = y[:, 8 * j : 8 * j + 8].reshape(a, f)

    def project(p, carry):
        r = pl.ds(pl.multiple_of(p * a, a), a)
        n = norm(xs[r], g[...])
        qs[r] = (mm(n, wq[...]) * (1.0 / (math.sqrt(D) * math.log(2.0)))).astype(BF16)
        ks[r] = mm(n, wk[...]).astype(BF16)
        vs[r] = mm(n, wv[...]).astype(BF16)
        return carry

    def attend(p, carry):
        r = pl.ds(pl.multiple_of(p * a, a), a)
        low = lax.broadcasted_iota(jnp.int32, (a, 2 * D), 1) < D
        zero = jnp.zeros((a, 2 * D), BF16)
        ones = jnp.ones((a, 2 * D), BF16)
        for hp in range(HEADS // 2):
            c = slice(hp * 2 * D, (hp + 1) * 2 * D)
            q, k = qs[r, c], ks[r, c]
            v = jnp.concatenate([vs[r, c], ones], axis=1)
            o = []
            for kh in (jnp.where(low, k, zero), jnp.where(low, zero, k)):
                l = mm_t(q, kh)
                e = jnp.exp2(l - jnp.max(l, axis=-1, keepdims=True)).astype(BF16)
                w = mm(e, v)
                o.append(w[:, : 2 * D] / w[:, 2 * D :])
            ms[r, c] = jnp.where(low, o[0], o[1]).astype(BF16)
        return carry

    def emit(p, carry):
        r = pl.ds(pl.multiple_of(p * a, a), a)
        xs[r] = xs[r] + mm(ms[r], wo[...])
        return carry

    lax.fori_loop(0, rows // 8, project, 0)
    lax.fori_loop(0, rows // 8, attend, 0)
    lax.fori_loop(0, rows // 8, emit, 0)
    for i in range(0, rows, 16):
        y = [xs[pl.ds((i // 8 + j) * a, a)].reshape(src, 8, f) for j in range(2)]
        out[:, i : i + 16] = jnp.concatenate(y, axis=1).astype(BF16)


def column(hc, g, wq, wk, wv, wo):
    src, rows, f = hc.shape
    m = src * rows
    return pl.pallas_call(
        column_kernel,
        out_shape=jax.ShapeDtypeStruct(hc.shape, BF16),
        scratch_shapes=[pltpu.VMEM((m, f), F32)] + [pltpu.VMEM((m, f), BF16)] * 5,
        compiler_params=PARAMS,
        name="column",
    )(*near(hc), *far(g, wq, wk, wv, wo))


def a2a(x):
    return lax.all_to_all(x, "seq", split_axis=0, concat_axis=0, tiled=True)


def shards(x, hg, wq, wk, wv, wo, vg, cq, ck, cv, co):
    S, N, F = x.shape
    hg = hg.reshape(1, F)
    vg = vg.reshape(1, F)
    barrier = lax.optimization_barrier

    def reduce(l):
        return a2a(l.reshape(SEQ, HEADS * N // SEQ, l.shape[-1]))

    xh = lax.ppermute(x, "res", XHI_SWAP)
    sib = lax.ppermute(x, "res", CORE_SWAP)

    def reduce_yz(l):
        half = SEQ // 2
        l = l.reshape(2, half, HEADS * N // SEQ, l.shape[-1]).transpose(1, 0, 2, 3)
        groups = [list(range(half)), list(range(half, SEQ))]
        l = lax.all_to_all(l, "seq", split_axis=0, concat_axis=0, tiled=True, axis_index_groups=groups)
        l = jnp.sum(l.astype(F32), axis=0)
        me = lax.axis_index("seq") // half
        other = lax.dynamic_index_in_dim(l, 1 - me, 0, keepdims=False).astype(BF16)
        mine = lax.dynamic_index_in_dim(l, me, 0, keepdims=False)
        return mine, lax.ppermute(other, "seq", [(i, (i + half) % SEQ) for i in range(SEQ)])

    q, l1 = logits(x, sib, hg, wk, wq=wq)
    r1 = reduce_yz(l1)
    xh, mine = barrier((xh, r1[0]))
    xhs = lax.ppermute(xh, "res", CORE_SWAP)
    (l2,) = logits(xh, xhs, hg, wk, q=q)
    l2, theirs = barrier((l2, r1[1]))
    r2 = jnp.sum(reduce(l2).astype(F32), axis=0)
    x_late, l2 = barrier((x, l2))
    v = values((x_late, sib, xh, xhs), hg, wv)
    scale = 1.0 / (math.sqrt(D) * math.sqrt(S * SEQ))
    tied = jnp.concatenate([mine + theirs.astype(F32), r2], axis=-1) * scale
    probs = jax.nn.softmax(tied, axis=-1).astype(BF16)
    probs = a2a(jnp.broadcast_to(probs[None], (SEQ,) + probs.shape)).reshape(HEADS, N, 4 * N)
    hid = mix(probs, v, x, wo)
    G = N // SEQ
    t = jnp.transpose(hid.reshape(S, SEQ, G, F), (1, 2, 0, 3)).reshape(SEQ, G * S, F)
    o = a2a(column(a2a(t), vg, cq, ck, cv, co))
    return jnp.transpose(o.reshape(SEQ, G, S, F), (2, 0, 1, 3)).reshape(S, N, F)


def solution(mesh):
    in_specs = (P("seq", "res", None),) + (P(),) * 10
    return jax.shard_map(shards, mesh=mesh, in_specs=in_specs, out_specs=P("seq", "res", None), check_vma=False)
```

```python
import functools
import math

import jax
import jax.numpy as jnp
from jax import lax
from jax.experimental import pallas as pl
from jax.experimental.pallas import tpu as pltpu
from jax.sharding import PartitionSpec as P

HEADS = 12
D = 64
SEQ = 32
CORE_SWAP = [(0, 1), (1, 0), (2, 3), (3, 2)]
XHI_SWAP = [(0, 2), (1, 3), (2, 0), (3, 1)]
F32 = jnp.float32
BF16 = jnp.bfloat16
PARAMS = pltpu.CompilerParams(vmem_limit_bytes=40 * 1024 * 1024)


def norm(x, gain):
    v = x.astype(F32)
    c = v - jnp.mean(v, axis=-1, keepdims=True)
    var = jnp.mean(c * c, axis=-1, keepdims=True)
    return (c * lax.rsqrt(var + 1e-05) * gain).astype(BF16)


def mm(a, b):
    return lax.dot_general(a, b, (((1,), (0,)), ((), ())), preferred_element_type=F32)


def mm_t(a, b):
    return lax.dot_general(a, b, (((1,), (1,)), ((), ())), preferred_element_type=F32)


def head(x, h):
    return x[:, h * D : (h + 1) * D]


def near(*arrays):
    return [pltpu.with_memory_space_constraint(a, pltpu.VMEM) for a in arrays]


def far(*arrays):
    return [pltpu.with_memory_space_constraint(a, pltpu.HBM) for a in arrays]


def whole(shape):
    return pl.BlockSpec(shape, lambda *_: (0,) * len(shape))


def pair(y, n, h):
    return jnp.concatenate([head(y[:n], h), head(y[n:], h)], axis=1)


def logits_kernel(first, *refs):
    if first:
        xa, xb, g, wk_h, wq_h, q, out, ks, wk, wq, sems = refs
        copies = [pltpu.make_async_copy(wk_h, wk, sems.at[0]), pltpu.make_async_copy(wq_h, wq, sems.at[1])]
    else:
        xa, xb, g, wk_h, q_h, out, ks, wk, q, sems = refs
        copies = [pltpu.make_async_copy(wk_h, wk, sems.at[0]), pltpu.make_async_copy(q_h, q, sems.at[1])]
    for c in copies:
        c.start()
    s, n, f = xa.shape
    na = norm(xa[...].reshape(s * n, f), g[...])
    nb = norm(xb[...].reshape(s * n, f), g[...])
    copies[0].wait()

    def put(ref, rows, y):
        for j in range(0, s, 2):
            z = y[j * n : (j + 2) * n]
            for h in range(HEADS):
                ref[h, rows, j * D : (j + 2) * D] = pair(z, n, h)

    put(ks, slice(0, n), mm(na, wk[...]).astype(BF16))
    put(ks, slice(n, 2 * n), mm(nb, wk[...]).astype(BF16))
    copies[1].wait()
    if first:
        put(q, slice(0, n), mm(na, wq[...]).astype(BF16))
    for h in range(HEADS):
        out[h] = mm_t(q[h], ks[h]).astype(BF16)


def logits(xa, xb, g, wk, wq=None, q=None):
    s, n, f = xa.shape
    first = q is None
    qshape = (HEADS, n, s * D)
    lshape = (HEADS, n, 2 * n)
    oshape = [jax.ShapeDtypeStruct(qshape, BF16), jax.ShapeDtypeStruct(lshape, BF16)]
    here = pl.BlockSpec(memory_space=pltpu.VMEM)
    there = pl.BlockSpec(memory_space=pl.ANY)
    return pl.pallas_call(
        functools.partial(logits_kernel, first),
        in_specs=[here, here, here, there, there],
        out_specs=[here, here] if first else [here],
        out_shape=oshape if first else oshape[1:],
        scratch_shapes=[
            pltpu.VMEM((HEADS, 2 * n, s * D), BF16),
            pltpu.VMEM(wk.shape, BF16),
            pltpu.VMEM(wq.shape if first else qshape, BF16),
            pltpu.SemaphoreType.DMA((2,)),
        ],
        compiler_params=PARAMS,
        name="logits",
    )(*(far(xa, xb) if first else near(xa, xb)), *far(g, wk, wq if first else q))


def values_kernel(*refs):
    xs, (g, wv, out) = refs[:-3], refs[-3:]
    at = 0
    for x in xs:
        n, f = x.shape[1:]
        v = mm(norm(x[...].reshape(2 * n, f), g[...]), wv[...]).astype(BF16)
        for h in range(HEADS):
            out[h, at : at + n] = pair(v, n, h)
        at += n


def values(pieces, g, wv):
    s, _, f = pieces[0].shape
    total = sum(p.shape[1] for p in pieces)
    specs = [pl.BlockSpec((2, p.shape[1], f), lambda t: (t, 0, 0)) for p in pieces]
    return pl.pallas_call(
        values_kernel,
        grid=(s // 2,),
        in_specs=specs + [whole(g.shape), whole(wv.shape)],
        out_specs=pl.BlockSpec((HEADS, total, 2 * D), lambda t: (0, 0, t)),
        out_shape=jax.ShapeDtypeStruct((HEADS, total, s * D), BF16),
        compiler_params=PARAMS,
        name="values",
    )(*far(*pieces, g, wv))


def mix_kernel(p, v_h, x_h, wo_h, out, ms, v, x, wo, sems):
    pairs = HEADS // 2
    s = x.shape[0]
    copies = [
        pltpu.make_async_copy(v_h.at[2 * t : 2 * t + 2], v.at[2 * t : 2 * t + 2], sems.at[t]) for t in range(pairs)
    ]
    copies += [pltpu.make_async_copy(x_h, x, sems.at[pairs]), pltpu.make_async_copy(wo_h, wo, sems.at[pairs + 1])]
    for c in copies:
        c.start()
    for t in range(pairs):
        copies[t].wait()
        o = [mm(p[2 * t + h], v[2 * t + h]).astype(BF16) for h in range(2)]
        for r in range(s):
            ms[r, :, t * 2 * D : (t + 1) * 2 * D] = jnp.concatenate([head(o[0], r), head(o[1], r)], axis=1)
    copies[pairs].wait()
    copies[pairs + 1].wait()
    y = mm(ms[...].reshape(-1, x.shape[2]), wo[...])
    out[...] = (x[...].astype(F32) + y.reshape(x.shape)).astype(BF16)


def mix(p, v, x, wo):
    s, n, f = x.shape
    here = pl.BlockSpec(memory_space=pltpu.VMEM)
    there = pl.BlockSpec(memory_space=pl.ANY)
    return pl.pallas_call(
        mix_kernel,
        in_specs=[here, there, there, there],
        out_specs=here,
        out_shape=jax.ShapeDtypeStruct(x.shape, BF16),
        scratch_shapes=[
            pltpu.VMEM((s, n, f), BF16),
            pltpu.VMEM(v.shape, BF16),
            pltpu.VMEM((s, n, f), BF16),
            pltpu.VMEM(wo.shape, BF16),
            pltpu.SemaphoreType.DMA((HEADS // 2 + 2,)),
        ],
        compiler_params=PARAMS,
        name="mix",
    )(*near(p), *far(v, x, wo))


def column_kernel(h_ref, g, *refs):
    away, (out, xs, ns, qs, ks, vs, ms, w, sems) = refs[:4], refs[4:]
    copies = [pltpu.make_async_copy(z, w.at[i], sems.at[i]) for i, z in enumerate(away)]
    for c in copies:
        c.start()
    src, rows, f = h_ref.shape
    a = src * 8
    for i in range(0, rows, 16):
        y = h_ref[:, i : i + 16].astype(F32)
        for j in range(2):
            xs[pl.ds((i // 8 + j) * a, a)] = y[:, 8 * j : 8 * j + 8].reshape(a, f)

    def normed(p, carry):
        r = pl.ds(pl.multiple_of(p * a, a), a)
        ns[r] = norm(xs[r], g[...])
        return carry

    def attend(p, carry):
        r = pl.ds(pl.multiple_of(p * a, a), a)
        low = lax.broadcasted_iota(jnp.int32, (a, 2 * D), 1) < D
        zero = jnp.zeros((a, 2 * D), BF16)
        one = jnp.ones((a, 2 * D), BF16)
        ones = jnp.concatenate([jnp.where(low, one, zero), jnp.where(low, zero, one)], axis=0)
        for hp in range(HEADS // 2):
            c = slice(hp * 2 * D, (hp + 1) * 2 * D)
            q, k, v = qs[r, c], ks[r, c], vs[r, c]
            k = jnp.concatenate([jnp.where(low, k, zero), jnp.where(low, zero, k)], axis=0)
            v = jnp.concatenate([jnp.where(low, v, zero), jnp.where(low, zero, v)], axis=0)
            l = mm_t(q, k)
            e = []
            for z in (l[:, :a], l[:, a:]):
                e.append(jnp.exp2(z - jnp.max(z, axis=-1, keepdims=True)).astype(BF16))
            w = mm(jnp.concatenate(e, axis=1), jnp.concatenate([v, ones], axis=1))
            ms[r, c] = (w[:, : 2 * D] / w[:, 2 * D :]).astype(BF16)
        return carry

    lax.fori_loop(0, rows // 8, normed, 0)
    n = ns[...]
    copies[0].wait()
    qs[...] = (mm(n, w[0]) * (1.0 / (math.sqrt(D) * math.log(2.0)))).astype(BF16)
    copies[1].wait()
    ks[...] = mm(n, w[1]).astype(BF16)
    copies[2].wait()
    vs[...] = mm(n, w[2]).astype(BF16)
    lax.fori_loop(0, rows // 8, attend, 0)
    copies[3].wait()
    xs[...] = xs[...] + mm(ms[...], w[3])
    for i in range(0, rows, 16):
        y = [xs[pl.ds((i // 8 + j) * a, a)].reshape(src, 8, f) for j in range(2)]
        out[:, i : i + 16] = jnp.concatenate(y, axis=1).astype(BF16)


def column(hc, g, wq, wk, wv, wo):
    src, rows, f = hc.shape
    m = src * rows
    return pl.pallas_call(
        column_kernel,
        in_specs=[pl.BlockSpec(memory_space=pltpu.VMEM)] * 2 + [pl.BlockSpec(memory_space=pl.ANY)] * 4,
        out_specs=pl.BlockSpec(memory_space=pltpu.VMEM),
        out_shape=jax.ShapeDtypeStruct(hc.shape, BF16),
        scratch_shapes=[pltpu.VMEM((m, f), F32)]
        + [pltpu.VMEM((m, f), BF16)] * 5
        + [pltpu.VMEM((4, f, f), BF16), pltpu.SemaphoreType.DMA((4,))],
        compiler_params=PARAMS,
        name="column",
    )(*near(hc), *far(g, wq, wk, wv, wo))


def a2a(x):
    return lax.all_to_all(x, "seq", split_axis=0, concat_axis=0, tiled=True)


def shards(x, hg, wq, wk, wv, wo, vg, cq, ck, cv, co):
    S, N, F = x.shape
    hg = hg.reshape(1, F)
    vg = vg.reshape(1, F)
    barrier = lax.optimization_barrier

    def reduce(l):
        return a2a(l.reshape(SEQ, HEADS * N // SEQ, l.shape[-1]))

    xh = lax.ppermute(x, "res", XHI_SWAP)
    sib = lax.ppermute(x, "res", CORE_SWAP)

    def reduce_yz(l):
        half = SEQ // 2
        l = l.reshape(2, half, HEADS * N // SEQ, l.shape[-1]).transpose(1, 0, 2, 3)
        groups = [list(range(half)), list(range(half, SEQ))]
        l = lax.all_to_all(l, "seq", split_axis=0, concat_axis=0, tiled=True, axis_index_groups=groups)
        l = jnp.sum(l.astype(F32), axis=0)
        me = lax.axis_index("seq") // half
        other = lax.dynamic_index_in_dim(l, 1 - me, 0, keepdims=False).astype(BF16)
        mine = lax.dynamic_index_in_dim(l, me, 0, keepdims=False)
        return mine, lax.ppermute(other, "seq", [(i, (i + half) % SEQ) for i in range(SEQ)])

    q, l1 = logits(x, sib, hg, wk, wq=wq)
    r1 = reduce_yz(l1)
    xh, mine = barrier((xh, r1[0]))
    xhs = lax.ppermute(xh, "res", CORE_SWAP)
    (l2,) = logits(xh, xhs, hg, wk, q=q)
    l2, theirs = barrier((l2, r1[1]))
    r2 = jnp.sum(reduce(l2).astype(F32), axis=0)
    x_late, l2 = barrier((x, l2))
    v = values((x_late, sib, xh, xhs), hg, wv)
    scale = 1.0 / (math.sqrt(D) * math.sqrt(S * SEQ))
    tied = jnp.concatenate([mine + theirs.astype(F32), r2], axis=-1) * scale
    probs = jax.nn.softmax(tied, axis=-1).astype(BF16)
    probs = a2a(jnp.broadcast_to(probs[None], (SEQ,) + probs.shape)).reshape(HEADS, N, 4 * N)
    hid = mix(probs, v, x, wo)
    G = N // SEQ
    t = jnp.transpose(hid.reshape(S, SEQ, G, F), (1, 2, 0, 3)).reshape(SEQ, G * S, F)
    o = a2a(column(a2a(t), vg, cq, ck, cv, co))
    return jnp.transpose(o.reshape(SEQ, G, S, F), (2, 0, 1, 3)).reshape(S, N, F)


def solution(mesh):
    in_specs = (P("seq", "res", None),) + (P(),) * 10
    return jax.shard_map(shards, mesh=mesh, in_specs=in_specs, out_specs=P("seq", "res", None), check_vma=False)
```

```python
import functools
import math

import jax
import jax.numpy as jnp
from jax import lax
from jax.experimental import pallas as pl
from jax.experimental.pallas import tpu as pltpu
from jax.sharding import PartitionSpec as P

HEADS = 12
D = 64
SEQ = 32
CORE_SWAP = [(0, 1), (1, 0), (2, 3), (3, 2)]
XHI_SWAP = [(0, 2), (1, 3), (2, 0), (3, 1)]
F32 = jnp.float32
BF16 = jnp.bfloat16
PARAMS = pltpu.CompilerParams(vmem_limit_bytes=40 * 1024 * 1024)


def norm(x, gain):
    v = x.astype(F32)
    c = v - jnp.mean(v, axis=-1, keepdims=True)
    var = jnp.mean(c * c, axis=-1, keepdims=True)
    return (c * lax.rsqrt(var + 1e-05) * gain).astype(BF16)


def mm(a, b):
    return lax.dot_general(a, b, (((1,), (0,)), ((), ())), preferred_element_type=F32)


def mm_t(a, b):
    return lax.dot_general(a, b, (((1,), (1,)), ((), ())), preferred_element_type=F32)


def head(x, h):
    return x[:, h * D : (h + 1) * D]


def near(*arrays):
    return [pltpu.with_memory_space_constraint(a, pltpu.VMEM) for a in arrays]


def far(*arrays):
    return [pltpu.with_memory_space_constraint(a, pltpu.HBM) for a in arrays]


def whole(shape):
    return pl.BlockSpec(shape, lambda *_: (0,) * len(shape))


def pair(y, n, h):
    return jnp.concatenate([head(y[:n], h), head(y[n:], h)], axis=1)


def logits_kernel(first, *refs):
    if first:
        xa, xb, g, wk_h, wq_h, q, out, ks, wk, wq, sems = refs
        copies = [pltpu.make_async_copy(wk_h, wk, sems.at[0]), pltpu.make_async_copy(wq_h, wq, sems.at[1])]
    else:
        xa, xb, g, wk_h, q_h, out, ks, wk, q, sems = refs
        copies = [pltpu.make_async_copy(wk_h, wk, sems.at[0]), pltpu.make_async_copy(q_h, q, sems.at[1])]
    for c in copies:
        c.start()
    s, n, f = xa.shape
    part = 4

    def put(ref, rows, at, y):
        for j in range(0, part, 2):
            z = y[j * n : (j + 2) * n]
            for h in range(HEADS):
                ref[h, rows, (at + j) * D : (at + j + 2) * D] = pair(z, n, h)

    own = []
    for at in range(0, s, part):
        for i, x in enumerate((xa, xb)):
            nx = norm(x[at : at + part].reshape(part * n, f), g[...])
            if i == 0:
                own.append(nx)
            if i == 0 and at == 0:
                copies[0].wait()
            put(ks, slice(i * n, (i + 1) * n), at, mm(nx, wk[...]).astype(BF16))
    copies[1].wait()
    if first:
        for i, nx in enumerate(own):
            put(q, slice(0, n), i * part, mm(nx, wq[...]).astype(BF16))
    for h in range(HEADS):
        out[h] = mm_t(q[h], ks[h]).astype(BF16)


def logits(xa, xb, g, wk, wq=None, q=None):
    s, n, f = xa.shape
    first = q is None
    qshape = (HEADS, n, s * D)
    lshape = (HEADS, n, 2 * n)
    oshape = [jax.ShapeDtypeStruct(qshape, BF16), jax.ShapeDtypeStruct(lshape, BF16)]
    here = pl.BlockSpec(memory_space=pltpu.VMEM)
    there = pl.BlockSpec(memory_space=pl.ANY)
    return pl.pallas_call(
        functools.partial(logits_kernel, first),
        in_specs=[here, here, here, there, there],
        out_specs=[here, here] if first else [here],
        out_shape=oshape if first else oshape[1:],
        scratch_shapes=[
            pltpu.VMEM((HEADS, 2 * n, s * D), BF16),
            pltpu.VMEM(wk.shape, BF16),
            pltpu.VMEM(wq.shape if first else qshape, BF16),
            pltpu.SemaphoreType.DMA((2,)),
        ],
        compiler_params=PARAMS,
        name="logits",
    )(*(far(xa, xb) if first else near(xa, xb)), *far(g, wk, wq if first else q))


def values_kernel(*refs):
    xs, (g, wv, out) = refs[:-3], refs[-3:]
    at = 0
    for x in xs:
        n, f = x.shape[1:]
        v = mm(norm(x[...].reshape(2 * n, f), g[...]), wv[...]).astype(BF16)
        for h in range(HEADS):
            out[h, at : at + n] = pair(v, n, h)
        at += n


def values(pieces, g, wv):
    s, _, f = pieces[0].shape
    total = sum(p.shape[1] for p in pieces)
    specs = [pl.BlockSpec((2, p.shape[1], f), lambda t: (t, 0, 0)) for p in pieces]
    return pl.pallas_call(
        values_kernel,
        grid=(s // 2,),
        in_specs=specs + [whole(g.shape), whole(wv.shape)],
        out_specs=pl.BlockSpec((HEADS, total, 2 * D), lambda t: (0, 0, t)),
        out_shape=jax.ShapeDtypeStruct((HEADS, total, s * D), BF16),
        compiler_params=PARAMS,
        name="values",
    )(*far(*pieces, g, wv))


def mix_kernel(p, v_h, x_h, wo_h, out, ms, v, x, wo, sems):
    pairs = HEADS // 2
    s = x.shape[0]
    copies = [
        pltpu.make_async_copy(v_h.at[2 * t : 2 * t + 2], v.at[2 * t : 2 * t + 2], sems.at[t]) for t in range(pairs)
    ]
    copies += [pltpu.make_async_copy(x_h, x, sems.at[pairs]), pltpu.make_async_copy(wo_h, wo, sems.at[pairs + 1])]
    for c in copies:
        c.start()
    for t in range(pairs):
        copies[t].wait()
        o = [mm(p[2 * t + h], v[2 * t + h]).astype(BF16) for h in range(2)]
        for r in range(s):
            ms[r, :, t * 2 * D : (t + 1) * 2 * D] = jnp.concatenate([head(o[0], r), head(o[1], r)], axis=1)
    copies[pairs].wait()
    copies[pairs + 1].wait()
    y = mm(ms[...].reshape(-1, x.shape[2]), wo[...])
    out[...] = (x[...].astype(F32) + y.reshape(x.shape)).astype(BF16)


def mix(p, v, x, wo):
    s, n, f = x.shape
    here = pl.BlockSpec(memory_space=pltpu.VMEM)
    there = pl.BlockSpec(memory_space=pl.ANY)
    return pl.pallas_call(
        mix_kernel,
        in_specs=[here, there, there, there],
        out_specs=here,
        out_shape=jax.ShapeDtypeStruct(x.shape, BF16),
        scratch_shapes=[
            pltpu.VMEM((s, n, f), BF16),
            pltpu.VMEM(v.shape, BF16),
            pltpu.VMEM((s, n, f), BF16),
            pltpu.VMEM(wo.shape, BF16),
            pltpu.SemaphoreType.DMA((HEADS // 2 + 2,)),
        ],
        compiler_params=PARAMS,
        name="mix",
    )(*near(p), *far(v, x, wo))


def column_kernel(h_ref, g, *refs):
    away, (out, xs, ns, qs, ks, vs, ms, w, sems) = refs[:4], refs[4:]
    copies = [pltpu.make_async_copy(z, w.at[i], sems.at[i]) for i, z in enumerate(away)]
    for c in copies:
        c.start()
    src, rows, f = h_ref.shape
    a = src * 8
    for i in range(0, rows, 16):
        y = h_ref[:, i : i + 16].astype(F32)
        for j in range(2):
            xs[pl.ds((i // 8 + j) * a, a)] = y[:, 8 * j : 8 * j + 8].reshape(a, f)

    def normed(p, carry):
        r = pl.ds(pl.multiple_of(p * a, a), a)
        ns[r] = norm(xs[r], g[...])
        return carry

    def attend(p, carry):
        r = pl.ds(pl.multiple_of(p * a, a), a)
        low = lax.broadcasted_iota(jnp.int32, (a, 2 * D), 1) < D
        zero = jnp.zeros((a, 2 * D), BF16)
        one = jnp.ones((a, 2 * D), BF16)
        ones = jnp.concatenate([jnp.where(low, one, zero), jnp.where(low, zero, one)], axis=0)
        for hp in range(HEADS // 2):
            c = slice(hp * 2 * D, (hp + 1) * 2 * D)
            q, k, v = qs[r, c], ks[r, c], vs[r, c]
            k = jnp.concatenate([jnp.where(low, k, zero), jnp.where(low, zero, k)], axis=0)
            v = jnp.concatenate([jnp.where(low, v, zero), jnp.where(low, zero, v)], axis=0)
            l = mm_t(q, k)
            e = []
            for z in (l[:, :a], l[:, a:]):
                e.append(jnp.exp2(z - jnp.max(z, axis=-1, keepdims=True)).astype(BF16))
            w = mm(jnp.concatenate(e, axis=1), jnp.concatenate([v, ones], axis=1))
            ms[r, c] = (w[:, : 2 * D] / w[:, 2 * D :]).astype(BF16)
        return carry

    for p in range(rows // 8):
        r = slice(p * a, (p + 1) * a)
        n = norm(xs[r], g[...])
        if p == 0:
            copies[0].wait()
        qs[r] = (mm(n, w[0]) * (1.0 / (math.sqrt(D) * math.log(2.0)))).astype(BF16)
        if p == 0:
            copies[1].wait()
        ks[r] = mm(n, w[1]).astype(BF16)
        if p == 0:
            copies[2].wait()
        vs[r] = mm(n, w[2]).astype(BF16)
    lax.fori_loop(0, rows // 8, attend, 0, unroll=2)
    copies[3].wait()
    xs[...] = xs[...] + mm(ms[...], w[3])
    for i in range(0, rows, 16):
        y = [xs[pl.ds((i // 8 + j) * a, a)].reshape(src, 8, f) for j in range(2)]
        out[:, i : i + 16] = jnp.concatenate(y, axis=1).astype(BF16)


def column(hc, g, wq, wk, wv, wo):
    src, rows, f = hc.shape
    m = src * rows
    return pl.pallas_call(
        column_kernel,
        in_specs=[pl.BlockSpec(memory_space=pltpu.VMEM)] * 2 + [pl.BlockSpec(memory_space=pl.ANY)] * 4,
        out_specs=pl.BlockSpec(memory_space=pltpu.VMEM),
        out_shape=jax.ShapeDtypeStruct(hc.shape, BF16),
        scratch_shapes=[pltpu.VMEM((m, f), F32)]
        + [pltpu.VMEM((m, f), BF16)] * 5
        + [pltpu.VMEM((4, f, f), BF16), pltpu.SemaphoreType.DMA((4,))],
        compiler_params=PARAMS,
        name="column",
    )(*near(hc), *far(g, wq, wk, wv, wo))


def a2a(x):
    return lax.all_to_all(x, "seq", split_axis=0, concat_axis=0, tiled=True)


def shards(x, hg, wq, wk, wv, wo, vg, cq, ck, cv, co):
    S, N, F = x.shape
    hg = hg.reshape(1, F)
    vg = vg.reshape(1, F)
    barrier = lax.optimization_barrier

    def reduce(l):
        return a2a(l.reshape(SEQ, HEADS * N // SEQ, l.shape[-1]))

    xh = lax.ppermute(x, "res", XHI_SWAP)
    sib = lax.ppermute(x, "res", CORE_SWAP)

    def reduce_yz(l):
        half = SEQ // 2
        l = l.reshape(2, half, HEADS * N // SEQ, l.shape[-1]).transpose(1, 0, 2, 3)
        groups = [list(range(half)), list(range(half, SEQ))]
        l = lax.all_to_all(l, "seq", split_axis=0, concat_axis=0, tiled=True, axis_index_groups=groups)
        l = jnp.sum(l.astype(F32), axis=0)
        me = lax.axis_index("seq") // half
        other = lax.dynamic_index_in_dim(l, 1 - me, 0, keepdims=False).astype(BF16)
        mine = lax.dynamic_index_in_dim(l, me, 0, keepdims=False)
        return mine, lax.ppermute(other, "seq", [(i, (i + half) % SEQ) for i in range(SEQ)])

    q, l1 = logits(x, sib, hg, wk, wq=wq)
    r1 = reduce_yz(l1)
    xh, mine = barrier((xh, r1[0]))
    xhs = lax.ppermute(xh, "res", CORE_SWAP)
    (l2,) = logits(xh, xhs, hg, wk, q=q)
    r2 = jnp.sum(reduce(l2).astype(F32), axis=0)
    x_late, l2 = barrier((x, l2))
    v = values((x_late, sib, xh, xhs), hg, wv)
    scale = 1.0 / (math.sqrt(D) * math.sqrt(S * SEQ))
    tied = jnp.concatenate([mine + r1[1].astype(F32), r2], axis=-1) * scale
    probs = jax.nn.softmax(tied, axis=-1).astype(BF16)
    probs = a2a(jnp.broadcast_to(probs[None], (SEQ,) + probs.shape)).reshape(HEADS, N, 4 * N)
    hid = mix(probs, v, x, wo)
    G = N // SEQ
    t = jnp.transpose(hid.reshape(S, SEQ, G, F), (1, 2, 0, 3)).reshape(SEQ, G * S, F)
    o = a2a(column(a2a(t), vg, cq, ck, cv, co))
    return jnp.transpose(o.reshape(SEQ, G, S, F), (2, 0, 1, 3)).reshape(S, N, F)


def solution(mesh):
    in_specs = (P("seq", "res", None),) + (P(),) * 10
    return jax.shard_map(shards, mesh=mesh, in_specs=in_specs, out_specs=P("seq", "res", None), check_vma=False)
```

```python
import functools
import math

import jax
import jax.numpy as jnp
from jax import lax
from jax.experimental import pallas as pl
from jax.experimental.pallas import tpu as pltpu
from jax.sharding import PartitionSpec as P

HEADS = 12
D = 64
SEQ = 32
CORE_SWAP = [(0, 1), (1, 0), (2, 3), (3, 2)]
XHI_SWAP = [(0, 2), (1, 3), (2, 0), (3, 1)]
F32 = jnp.float32
BF16 = jnp.bfloat16
PARAMS = pltpu.CompilerParams(vmem_limit_bytes=40 * 1024 * 1024)


def norm(x, gain):
    v = x.astype(F32)
    c = v - jnp.mean(v, axis=-1, keepdims=True)
    var = jnp.mean(c * c, axis=-1, keepdims=True)
    return (c * lax.rsqrt(var + 1e-05) * gain).astype(BF16)


def mm(a, b):
    return lax.dot_general(a, b, (((1,), (0,)), ((), ())), preferred_element_type=F32)


def mm_t(a, b):
    return lax.dot_general(a, b, (((1,), (1,)), ((), ())), preferred_element_type=F32)


def head(x, h):
    return x[:, h * D : (h + 1) * D]


def near(*arrays):
    return [pltpu.with_memory_space_constraint(a, pltpu.VMEM) for a in arrays]


def far(*arrays):
    return [pltpu.with_memory_space_constraint(a, pltpu.HBM) for a in arrays]


def whole(shape):
    return pl.BlockSpec(shape, lambda *_: (0,) * len(shape))


def pair(y, n, h):
    return jnp.concatenate([head(y[:n], h), head(y[n:], h)], axis=1)


def logits_kernel(first, *refs):
    if first:
        xa, xb, g, wk_h, wq_h, q, out, ks, wk, wq, sems = refs
        copies = [pltpu.make_async_copy(wk_h, wk, sems.at[0]), pltpu.make_async_copy(wq_h, wq, sems.at[1])]
    else:
        xa, xb, g, wk_h, q_h, out, ks, wk, q, sems = refs
        copies = [pltpu.make_async_copy(wk_h, wk, sems.at[0]), pltpu.make_async_copy(q_h, q, sems.at[1])]
    for c in copies:
        c.start()
    s, n, f = xa.shape
    part = 4

    def put(ref, rows, at, y):
        for j in range(0, part, 2):
            z = y[j * n : (j + 2) * n]
            for h in range(HEADS):
                ref[h, rows, (at + j) * D : (at + j + 2) * D] = pair(z, n, h)

    own = []
    for at in range(0, s, part):
        for i, x in enumerate((xa, xb)):
            nx = norm(x[at : at + part].reshape(part * n, f), g[...])
            if i == 0:
                own.append(nx)
            if i == 0 and at == 0:
                copies[0].wait()
            put(ks, slice(i * n, (i + 1) * n), at, mm(nx, wk[...]).astype(BF16))
    copies[1].wait()
    if first:
        for i, nx in enumerate(own):
            put(q, slice(0, n), i * part, mm(nx, wq[...]).astype(BF16))
    for h in range(HEADS):
        out[h] = mm_t(q[h], ks[h]).astype(BF16)


def logits(xa, xb, g, wk, wq=None, q=None):
    s, n, f = xa.shape
    first = q is None
    qshape = (HEADS, n, s * D)
    lshape = (HEADS, n, 2 * n)
    oshape = [jax.ShapeDtypeStruct(qshape, BF16), jax.ShapeDtypeStruct(lshape, BF16)]
    here = pl.BlockSpec(memory_space=pltpu.VMEM)
    there = pl.BlockSpec(memory_space=pl.ANY)
    return pl.pallas_call(
        functools.partial(logits_kernel, first),
        in_specs=[here, here, here, there, there],
        out_specs=[here, here] if first else [here],
        out_shape=oshape if first else oshape[1:],
        scratch_shapes=[
            pltpu.VMEM((HEADS, 2 * n, s * D), BF16),
            pltpu.VMEM(wk.shape, BF16),
            pltpu.VMEM(wq.shape if first else qshape, BF16),
            pltpu.SemaphoreType.DMA((2,)),
        ],
        compiler_params=PARAMS,
        name="logits",
    )(*(far(xa, xb) if first else near(xa, xb)), *far(g, wk, wq if first else q))


def values_kernel(*refs):
    xs, (g, wv, out) = refs[:-3], refs[-3:]
    at = 0
    for x in xs:
        n, f = x.shape[1:]
        v = mm(norm(x[...].reshape(2 * n, f), g[...]), wv[...]).astype(BF16)
        for h in range(HEADS):
            out[h, at : at + n] = pair(v, n, h)
        at += n


def values(pieces, g, wv):
    s, _, f = pieces[0].shape
    total = sum(p.shape[1] for p in pieces)
    specs = [pl.BlockSpec((2, p.shape[1], f), lambda t: (t, 0, 0)) for p in pieces]
    return pl.pallas_call(
        values_kernel,
        grid=(s // 2,),
        in_specs=specs + [whole(g.shape), whole(wv.shape)],
        out_specs=pl.BlockSpec((HEADS, total, 2 * D), lambda t: (0, 0, t)),
        out_shape=jax.ShapeDtypeStruct((HEADS, total, s * D), BF16),
        compiler_params=PARAMS,
        name="values",
    )(*far(*pieces, g, wv))


def mix_kernel(p, v_h, x_h, wo_h, out, ms, v, x, wo, sems):
    pairs = HEADS // 2
    s = x.shape[0]
    copies = [
        pltpu.make_async_copy(v_h.at[2 * t : 2 * t + 2], v.at[2 * t : 2 * t + 2], sems.at[t]) for t in range(pairs)
    ]
    copies += [pltpu.make_async_copy(x_h, x, sems.at[pairs]), pltpu.make_async_copy(wo_h, wo, sems.at[pairs + 1])]
    for c in copies:
        c.start()
    for t in range(pairs):
        copies[t].wait()
        o = [mm(p[2 * t + h], v[2 * t + h]).astype(BF16) for h in range(2)]
        for r in range(s):
            ms[r, :, t * 2 * D : (t + 1) * 2 * D] = jnp.concatenate([head(o[0], r), head(o[1], r)], axis=1)
    copies[pairs].wait()
    copies[pairs + 1].wait()
    y = mm(ms[...].reshape(-1, x.shape[2]), wo[...])
    out[...] = (x[...].astype(F32) + y.reshape(x.shape)).astype(BF16)


def mix(p, v, x, wo):
    s, n, f = x.shape
    here = pl.BlockSpec(memory_space=pltpu.VMEM)
    there = pl.BlockSpec(memory_space=pl.ANY)
    return pl.pallas_call(
        mix_kernel,
        in_specs=[here, there, there, there],
        out_specs=here,
        out_shape=jax.ShapeDtypeStruct(x.shape, BF16),
        scratch_shapes=[
            pltpu.VMEM((s, n, f), BF16),
            pltpu.VMEM(v.shape, BF16),
            pltpu.VMEM((s, n, f), BF16),
            pltpu.VMEM(wo.shape, BF16),
            pltpu.SemaphoreType.DMA((HEADS // 2 + 2,)),
        ],
        compiler_params=PARAMS,
        name="mix",
    )(*near(p), *far(v, x, wo))


def column_kernel(h_ref, g, *refs):
    away, (out, xs, ns, qs, ks, vs, ms, w, sems) = refs[:4], refs[4:]
    copies = [pltpu.make_async_copy(z, w.at[i], sems.at[i]) for i, z in enumerate(away)]
    for c in copies:
        c.start()
    src, rows, f = h_ref.shape
    a = src * 8
    for i in range(0, rows, 16):
        y = h_ref[:, i : i + 16].astype(F32)
        for j in range(2):
            xs[pl.ds((i // 8 + j) * a, a)] = y[:, 8 * j : 8 * j + 8].reshape(a, f)

    def normed(p, carry):
        r = pl.ds(pl.multiple_of(p * a, a), a)
        ns[r] = norm(xs[r], g[...])
        return carry

    def attend(p, carry):
        r = pl.ds(pl.multiple_of(p * a, a), a)
        low = lax.broadcasted_iota(jnp.int32, (a, 2 * D), 1) < D
        zero = jnp.zeros((a, 2 * D), BF16)
        one = jnp.ones((a, 2 * D), BF16)
        ones = jnp.concatenate([jnp.where(low, one, zero), jnp.where(low, zero, one)], axis=0)
        for hp in range(HEADS // 2):
            c = slice(hp * 2 * D, (hp + 1) * 2 * D)
            q, k, v = qs[r, c], ks[r, c], vs[r, c]
            k = jnp.concatenate([jnp.where(low, k, zero), jnp.where(low, zero, k)], axis=0)
            v = jnp.concatenate([jnp.where(low, v, zero), jnp.where(low, zero, v)], axis=0)
            l = mm_t(q, k)
            e = []
            for z in (l[:, :a], l[:, a:]):
                e.append(jnp.exp2(z - jnp.max(z, axis=-1, keepdims=True)).astype(BF16))
            w = mm(jnp.concatenate(e, axis=1), jnp.concatenate([v, ones], axis=1))
            ms[r, c] = (w[:, : 2 * D] / w[:, 2 * D :]).astype(BF16)
        return carry

    for p in range(rows // 8):
        r = slice(p * a, (p + 1) * a)
        n = norm(xs[r], g[...])
        if p == 0:
            copies[0].wait()
        qs[r] = (mm(n, w[0]) * (1.0 / (math.sqrt(D) * math.log(2.0)))).astype(BF16)
        if p == 0:
            copies[1].wait()
        ks[r] = mm(n, w[1]).astype(BF16)
        if p == 0:
            copies[2].wait()
        vs[r] = mm(n, w[2]).astype(BF16)
    lax.fori_loop(0, rows // 8, attend, 0, unroll=2)
    copies[3].wait()
    xs[...] = xs[...] + mm(ms[...], w[3])
    for i in range(0, rows, 16):
        y = [xs[pl.ds((i // 8 + j) * a, a)].reshape(src, 8, f) for j in range(2)]
        out[:, i : i + 16] = jnp.concatenate(y, axis=1).astype(BF16)


def column(hc, g, wq, wk, wv, wo):
    src, rows, f = hc.shape
    m = src * rows
    return pl.pallas_call(
        column_kernel,
        in_specs=[pl.BlockSpec(memory_space=pltpu.VMEM)] * 2 + [pl.BlockSpec(memory_space=pl.ANY)] * 4,
        out_specs=pl.BlockSpec(memory_space=pltpu.VMEM),
        out_shape=jax.ShapeDtypeStruct(hc.shape, BF16),
        scratch_shapes=[pltpu.VMEM((m, f), F32)]
        + [pltpu.VMEM((m, f), BF16)] * 5
        + [pltpu.VMEM((4, f, f), BF16), pltpu.SemaphoreType.DMA((4,))],
        compiler_params=PARAMS,
        name="column",
    )(*near(hc), *far(g, wq, wk, wv, wo))


def a2a(x):
    return lax.all_to_all(x, "seq", split_axis=0, concat_axis=0, tiled=True)


def shards(x, hg, wq, wk, wv, wo, vg, cq, ck, cv, co):
    S, N, F = x.shape
    hg = hg.reshape(1, F)
    vg = vg.reshape(1, F)
    barrier = lax.optimization_barrier

    def reduce(l):
        return a2a(l.reshape(SEQ, HEADS * N // SEQ, l.shape[-1]))

    xh = lax.ppermute(x, "res", XHI_SWAP)
    sib = lax.ppermute(x, "res", CORE_SWAP)

    def reduce_yz(l):
        half = SEQ // 2
        l = l.reshape(2, half, HEADS * N // SEQ, l.shape[-1]).transpose(1, 0, 2, 3)
        groups = [list(range(half)), list(range(half, SEQ))]
        l = lax.all_to_all(l, "seq", split_axis=0, concat_axis=0, tiled=True, axis_index_groups=groups)
        l = jnp.sum(l.astype(F32), axis=0)
        me = lax.axis_index("seq") // half
        other = lax.dynamic_index_in_dim(l, 1 - me, 0, keepdims=False).astype(BF16)
        mine = lax.dynamic_index_in_dim(l, me, 0, keepdims=False)
        return mine, lax.ppermute(other, "seq", [(i, (i + half) % SEQ) for i in range(SEQ)])

    q, l1 = logits(x, sib, hg, wk, wq=wq)
    r1 = reduce_yz(l1)
    xh, mine = barrier((xh, r1[0]))
    xhs = lax.ppermute(xh, "res", CORE_SWAP)
    (l2,) = logits(xh, xhs, hg, wk, q=q)
    def late(l):
        early = values((x, sib, xh, xhs), hg, wv)
        return l + early[0, 0, 0] * 0

    l2 = lax.cond(lax.axis_index("res") % 2 == 1, late, lambda l: l, l2)
    r2 = jnp.sum(reduce(l2).astype(F32), axis=0)
    x_late, l2 = barrier((x, l2))
    v = values((x_late, sib, xh, xhs), hg, wv)
    scale = 1.0 / (math.sqrt(D) * math.sqrt(S * SEQ))
    tied = jnp.concatenate([mine + r1[1].astype(F32), r2], axis=-1) * scale
    probs = jax.nn.softmax(tied, axis=-1).astype(BF16)
    probs = a2a(jnp.broadcast_to(probs[None], (SEQ,) + probs.shape)).reshape(HEADS, N, 4 * N)
    hid = mix(probs, v, x, wo)
    G = N // SEQ
    t = jnp.transpose(hid.reshape(S, SEQ, G, F), (1, 2, 0, 3)).reshape(SEQ, G * S, F)
    o = a2a(column(a2a(t), vg, cq, ck, cv, co))
    return jnp.transpose(o.reshape(SEQ, G, S, F), (2, 0, 1, 3)).reshape(S, N, F)


def solution(mesh):
    in_specs = (P("seq", "res", None),) + (P(),) * 10
    return jax.shard_map(shards, mesh=mesh, in_specs=in_specs, out_specs=P("seq", "res", None), check_vma=False)
```

```python
import functools
import math

import jax
import jax.numpy as jnp
from jax import lax
from jax.experimental import pallas as pl
from jax.experimental.pallas import tpu as pltpu
from jax.sharding import PartitionSpec as P

HEADS = 12
D = 64
SEQ = 32
CORE_SWAP = [(0, 1), (1, 0), (2, 3), (3, 2)]
XHI_SWAP = [(0, 2), (1, 3), (2, 0), (3, 1)]
F32 = jnp.float32
BF16 = jnp.bfloat16
PARAMS = pltpu.CompilerParams(vmem_limit_bytes=40 * 1024 * 1024)


def norm(x, gain):
    v = x.astype(F32)
    c = v - jnp.mean(v, axis=-1, keepdims=True)
    var = jnp.mean(c * c, axis=-1, keepdims=True)
    return (c * lax.rsqrt(var + 1e-05) * gain).astype(BF16)


def mm(a, b):
    return lax.dot_general(a, b, (((1,), (0,)), ((), ())), preferred_element_type=F32)


def mm_t(a, b):
    return lax.dot_general(a, b, (((1,), (1,)), ((), ())), preferred_element_type=F32)


def head(x, h):
    return x[:, h * D : (h + 1) * D]


def near(*arrays):
    return [pltpu.with_memory_space_constraint(a, pltpu.VMEM) for a in arrays]


def far(*arrays):
    return [pltpu.with_memory_space_constraint(a, pltpu.HBM) for a in arrays]


def whole(shape):
    return pl.BlockSpec(shape, lambda *_: (0,) * len(shape))


def pair(y, n, h):
    return jnp.concatenate([head(y[:n], h), head(y[n:], h)], axis=1)


def logits_kernel(first, *refs):
    if first:
        xa, xb, g, wk_h, wq_h, q, out, ks, wk, wq, sems = refs
        copies = [pltpu.make_async_copy(wk_h, wk, sems.at[0]), pltpu.make_async_copy(wq_h, wq, sems.at[1])]
    else:
        xa, xb, g, wk_h, q_h, out, ks, wk, q, sems = refs
        copies = [pltpu.make_async_copy(wk_h, wk, sems.at[0]), pltpu.make_async_copy(q_h, q, sems.at[1])]
    for c in copies:
        c.start()
    s, n, f = xa.shape
    part = 4

    def put(ref, rows, at, y):
        for j in range(0, part, 2):
            z = y[j * n : (j + 2) * n]
            for h in range(HEADS):
                ref[h, rows, (at + j) * D : (at + j + 2) * D] = pair(z, n, h)

    own = []
    for at in range(0, s, part):
        for i, x in enumerate((xa, xb)):
            nx = norm(x[at : at + part].reshape(part * n, f), g[...])
            if i == 0:
                own.append(nx)
            if i == 0 and at == 0:
                copies[0].wait()
            put(ks, slice(i * n, (i + 1) * n), at, mm(nx, wk[...]).astype(BF16))
    copies[1].wait()
    if first:
        for i, nx in enumerate(own):
            put(q, slice(0, n), i * part, mm(nx, wq[...]).astype(BF16))
    for h in range(HEADS):
        out[h] = mm_t(q[h], ks[h]).astype(BF16)


def logits(xa, xb, g, wk, wq=None, q=None):
    s, n, f = xa.shape
    first = q is None
    qshape = (HEADS, n, s * D)
    lshape = (HEADS, n, 2 * n)
    oshape = [jax.ShapeDtypeStruct(qshape, BF16), jax.ShapeDtypeStruct(lshape, BF16)]
    here = pl.BlockSpec(memory_space=pltpu.VMEM)
    there = pl.BlockSpec(memory_space=pl.ANY)
    return pl.pallas_call(
        functools.partial(logits_kernel, first),
        in_specs=[here, here, here, there, there],
        out_specs=[here, here] if first else [here],
        out_shape=oshape if first else oshape[1:],
        scratch_shapes=[
            pltpu.VMEM((HEADS, 2 * n, s * D), BF16),
            pltpu.VMEM(wk.shape, BF16),
            pltpu.VMEM(wq.shape if first else qshape, BF16),
            pltpu.SemaphoreType.DMA((2,)),
        ],
        compiler_params=PARAMS,
        name="logits",
    )(*(far(xa, xb) if first else near(xa, xb)), *far(g, wk, wq if first else q))


def values_kernel(*refs):
    xs, (g, wv, out) = refs[:-3], refs[-3:]
    at = 0
    for x in xs:
        n, f = x.shape[1:]
        v = mm(norm(x[...].reshape(2 * n, f), g[...]), wv[...]).astype(BF16)
        for h in range(HEADS):
            out[h, at : at + n] = pair(v, n, h)
        at += n


def values(pieces, g, wv):
    s, _, f = pieces[0].shape
    total = sum(p.shape[1] for p in pieces)
    specs = [pl.BlockSpec((2, p.shape[1], f), lambda t: (t, 0, 0)) for p in pieces]
    return pl.pallas_call(
        values_kernel,
        grid=(s // 2,),
        in_specs=specs + [whole(g.shape), whole(wv.shape)],
        out_specs=pl.BlockSpec((HEADS, total, 2 * D), lambda t: (0, 0, t)),
        out_shape=pltpu.HBM((HEADS, total, s * D), BF16),
        compiler_params=PARAMS,
        name="values",
    )(*far(*pieces, g, wv))


def mix_kernel(p, v_h, x_h, wo_h, out, ms, v, x, wo, sems):
    pairs = HEADS // 2
    s = x.shape[0]
    copies = [
        pltpu.make_async_copy(v_h.at[2 * t : 2 * t + 2], v.at[2 * t : 2 * t + 2], sems.at[t]) for t in range(pairs)
    ]
    copies += [pltpu.make_async_copy(x_h, x, sems.at[pairs]), pltpu.make_async_copy(wo_h, wo, sems.at[pairs + 1])]
    for c in copies:
        c.start()
    for t in range(pairs):
        copies[t].wait()
        o = [mm(p[2 * t + h], v[2 * t + h]).astype(BF16) for h in range(2)]
        for r in range(s):
            ms[r, :, t * 2 * D : (t + 1) * 2 * D] = jnp.concatenate([head(o[0], r), head(o[1], r)], axis=1)
    copies[pairs].wait()
    copies[pairs + 1].wait()
    y = mm(ms[...].reshape(-1, x.shape[2]), wo[...])
    out[...] = (x[...].astype(F32) + y.reshape(x.shape)).astype(BF16)


def mix(p, v, x, wo):
    s, n, f = x.shape
    here = pl.BlockSpec(memory_space=pltpu.VMEM)
    there = pl.BlockSpec(memory_space=pl.ANY)
    return pl.pallas_call(
        mix_kernel,
        in_specs=[here, there, there, there],
        out_specs=here,
        out_shape=jax.ShapeDtypeStruct(x.shape, BF16),
        scratch_shapes=[
            pltpu.VMEM((s, n, f), BF16),
            pltpu.VMEM(v.shape, BF16),
            pltpu.VMEM((s, n, f), BF16),
            pltpu.VMEM(wo.shape, BF16),
            pltpu.SemaphoreType.DMA((HEADS // 2 + 2,)),
        ],
        compiler_params=PARAMS,
        name="mix",
    )(*near(p), *far(v, x, wo))


def column_kernel(h_ref, g, *refs):
    away, (out, xs, ns, qs, ks, vs, ms, w, sems) = refs[:4], refs[4:]
    copies = [pltpu.make_async_copy(z, w.at[i], sems.at[i]) for i, z in enumerate(away)]
    for c in copies:
        c.start()
    src, rows, f = h_ref.shape
    a = src * 8
    for i in range(0, rows, 16):
        y = h_ref[:, i : i + 16].astype(F32)
        for j in range(2):
            xs[pl.ds((i // 8 + j) * a, a)] = y[:, 8 * j : 8 * j + 8].reshape(a, f)

    def normed(p, carry):
        r = pl.ds(pl.multiple_of(p * a, a), a)
        ns[r] = norm(xs[r], g[...])
        return carry

    def attend(p, carry):
        r = pl.ds(pl.multiple_of(p * a, a), a)
        low = lax.broadcasted_iota(jnp.int32, (a, 2 * D), 1) < D
        zero = jnp.zeros((a, 2 * D), BF16)
        one = jnp.ones((a, 2 * D), BF16)
        ones = jnp.concatenate([jnp.where(low, one, zero), jnp.where(low, zero, one)], axis=0)
        for hp in range(HEADS // 2):
            c = slice(hp * 2 * D, (hp + 1) * 2 * D)
            q, k, v = qs[r, c], ks[r, c], vs[r, c]
            k = jnp.concatenate([jnp.where(low, k, zero), jnp.where(low, zero, k)], axis=0)
            v = jnp.concatenate([jnp.where(low, v, zero), jnp.where(low, zero, v)], axis=0)
            l = mm_t(q, k)
            e = []
            for z in (l[:, :a], l[:, a:]):
                e.append(jnp.exp2(z - jnp.max(z, axis=-1, keepdims=True)).astype(BF16))
            w = mm(jnp.concatenate(e, axis=1), jnp.concatenate([v, ones], axis=1))
            ms[r, c] = (w[:, : 2 * D] / w[:, 2 * D :]).astype(BF16)
        return carry

    for p in range(rows // 8):
        r = slice(p * a, (p + 1) * a)
        n = norm(xs[r], g[...])
        if p == 0:
            copies[0].wait()
        qs[r] = (mm(n, w[0]) * (1.0 / (math.sqrt(D) * math.log(2.0)))).astype(BF16)
        if p == 0:
            copies[1].wait()
        ks[r] = mm(n, w[1]).astype(BF16)
        if p == 0:
            copies[2].wait()
        vs[r] = mm(n, w[2]).astype(BF16)
    lax.fori_loop(0, rows // 8, attend, 0, unroll=2)
    copies[3].wait()
    xs[...] = xs[...] + mm(ms[...], w[3])
    for i in range(0, rows, 16):
        y = [xs[pl.ds((i // 8 + j) * a, a)].reshape(src, 8, f) for j in range(2)]
        out[:, i : i + 16] = jnp.concatenate(y, axis=1).astype(BF16)


def column(hc, g, wq, wk, wv, wo):
    src, rows, f = hc.shape
    m = src * rows
    return pl.pallas_call(
        column_kernel,
        in_specs=[pl.BlockSpec(memory_space=pltpu.VMEM)] * 2 + [pl.BlockSpec(memory_space=pl.ANY)] * 4,
        out_specs=pl.BlockSpec(memory_space=pltpu.VMEM),
        out_shape=jax.ShapeDtypeStruct(hc.shape, BF16),
        scratch_shapes=[pltpu.VMEM((m, f), F32)]
        + [pltpu.VMEM((m, f), BF16)] * 5
        + [pltpu.VMEM((4, f, f), BF16), pltpu.SemaphoreType.DMA((4,))],
        compiler_params=PARAMS,
        name="column",
    )(*near(hc), *far(g, wq, wk, wv, wo))


def a2a(x):
    return lax.all_to_all(x, "seq", split_axis=0, concat_axis=0, tiled=True)


def shards(x, hg, wq, wk, wv, wo, vg, cq, ck, cv, co):
    S, N, F = x.shape
    hg = hg.reshape(1, F)
    vg = vg.reshape(1, F)
    barrier = lax.optimization_barrier

    def reduce(l):
        return a2a(l.reshape(SEQ, HEADS * N // SEQ, l.shape[-1]))

    xh = lax.ppermute(x, "res", XHI_SWAP)
    sib = lax.ppermute(x, "res", CORE_SWAP)

    def reduce_yz(l):
        half = SEQ // 2
        l = l.reshape(2, half, HEADS * N // SEQ, l.shape[-1]).transpose(1, 0, 2, 3)
        groups = [list(range(half)), list(range(half, SEQ))]
        l = lax.all_to_all(l, "seq", split_axis=0, concat_axis=0, tiled=True, axis_index_groups=groups)
        l = jnp.sum(l.astype(F32), axis=0)
        me = lax.axis_index("seq") // half
        other = lax.dynamic_index_in_dim(l, 1 - me, 0, keepdims=False).astype(BF16)
        mine = lax.dynamic_index_in_dim(l, me, 0, keepdims=False)
        return mine, lax.ppermute(other, "seq", [(i, (i + half) % SEQ) for i in range(SEQ)])

    q, l1 = logits(x, sib, hg, wk, wq=wq)
    r1 = reduce_yz(l1)
    xh, mine = barrier((xh, r1[0]))
    xhs = lax.ppermute(xh, "res", CORE_SWAP)
    (l2,) = logits(xh, xhs, hg, wk, q=q)
    odd = lax.axis_index("res") % 2 == 1
    early = lax.cond(
        odd, lambda l: values((x, sib, xh, xhs), hg, wv)[0, 0, 0] + l * 0, lambda l: jnp.zeros_like(l), l2[0, 0, 0]
    )
    l2, early = barrier((l2, early))
    r2 = jnp.sum(reduce(l2).astype(F32), axis=0)
    x_late, l2 = barrier((x, l2))
    v = values((x_late, sib, xh, xhs), hg, wv)
    scale = 1.0 / (math.sqrt(D) * math.sqrt(S * SEQ))
    tied = jnp.concatenate([mine + r1[1].astype(F32), r2 + early.astype(F32) * 0], axis=-1) * scale
    probs = jax.nn.softmax(tied, axis=-1).astype(BF16)
    probs = a2a(jnp.broadcast_to(probs[None], (SEQ,) + probs.shape)).reshape(HEADS, N, 4 * N)
    hid = mix(probs, v, x, wo)
    G = N // SEQ
    t = jnp.transpose(hid.reshape(S, SEQ, G, F), (1, 2, 0, 3)).reshape(SEQ, G * S, F)
    o = a2a(column(a2a(t), vg, cq, ck, cv, co))
    return jnp.transpose(o.reshape(SEQ, G, S, F), (2, 0, 1, 3)).reshape(S, N, F)


def solution(mesh):
    in_specs = (P("seq", "res", None),) + (P(),) * 10
    return jax.shard_map(shards, mesh=mesh, in_specs=in_specs, out_specs=P("seq", "res", None), check_vma=False)
```

```python
import functools
import math

import jax
import jax.numpy as jnp
from jax import lax
from jax.experimental import pallas as pl
from jax.experimental.pallas import tpu as pltpu
from jax.sharding import PartitionSpec as P

HEADS = 12
D = 64
SEQ = 32
CORE_SWAP = [(0, 1), (1, 0), (2, 3), (3, 2)]
XHI_SWAP = [(0, 2), (1, 3), (2, 0), (3, 1)]
F32 = jnp.float32
BF16 = jnp.bfloat16
PARAMS = pltpu.CompilerParams(vmem_limit_bytes=40 * 1024 * 1024)


def norm(x, gain):
    v = x.astype(F32)
    c = v - jnp.mean(v, axis=-1, keepdims=True)
    var = jnp.mean(c * c, axis=-1, keepdims=True)
    return (c * lax.rsqrt(var + 1e-05) * gain).astype(BF16)


def mm(a, b):
    return lax.dot_general(a, b, (((1,), (0,)), ((), ())), preferred_element_type=F32)


def mm_t(a, b):
    return lax.dot_general(a, b, (((1,), (1,)), ((), ())), preferred_element_type=F32)


def head(x, h):
    return x[:, h * D : (h + 1) * D]


def near(*arrays):
    return [pltpu.with_memory_space_constraint(a, pltpu.VMEM) for a in arrays]


def far(*arrays):
    return [pltpu.with_memory_space_constraint(a, pltpu.HBM) for a in arrays]


def whole(shape):
    return pl.BlockSpec(shape, lambda *_: (0,) * len(shape))


def pair(y, n, h):
    return jnp.concatenate([head(y[:n], h), head(y[n:], h)], axis=1)


def logits_kernel(first, *refs):
    if first:
        xa, xb, g, wk_h, wq_h, q, out, ks, wk, wq, sems = refs
        copies = [pltpu.make_async_copy(wk_h, wk, sems.at[0]), pltpu.make_async_copy(wq_h, wq, sems.at[1])]
    else:
        xa, xb, g, wk_h, q_h, out, ks, wk, q, sems = refs
        copies = [pltpu.make_async_copy(wk_h, wk, sems.at[0]), pltpu.make_async_copy(q_h, q, sems.at[1])]
    for c in copies:
        c.start()
    s, n, f = xa.shape
    part = 4

    def put(ref, rows, at, y):
        for j in range(0, part, 2):
            z = y[j * n : (j + 2) * n]
            for h in range(HEADS):
                ref[h, rows, (at + j) * D : (at + j + 2) * D] = pair(z, n, h)

    own = []
    for at in range(0, s, part):
        for i, x in enumerate((xa, xb)):
            nx = norm(x[at : at + part].reshape(part * n, f), g[...])
            if i == 0:
                own.append(nx)
            if i == 0 and at == 0:
                copies[0].wait()
            put(ks, slice(i * n, (i + 1) * n), at, mm(nx, wk[...]).astype(BF16))
    copies[1].wait()
    if first:
        for i, nx in enumerate(own):
            put(q, slice(0, n), i * part, mm(nx, wq[...]).astype(BF16))
    for h in range(HEADS):
        out[h] = mm_t(q[h], ks[h]).astype(BF16)


def logits(xa, xb, g, wk, wq=None, q=None):
    s, n, f = xa.shape
    first = q is None
    qshape = (HEADS, n, s * D)
    lshape = (HEADS, n, 2 * n)
    oshape = [jax.ShapeDtypeStruct(qshape, BF16), jax.ShapeDtypeStruct(lshape, BF16)]
    here = pl.BlockSpec(memory_space=pltpu.VMEM)
    there = pl.BlockSpec(memory_space=pl.ANY)
    return pl.pallas_call(
        functools.partial(logits_kernel, first),
        in_specs=[here, here, here, there, there],
        out_specs=[here, here] if first else [here],
        out_shape=oshape if first else oshape[1:],
        scratch_shapes=[
            pltpu.VMEM((HEADS, 2 * n, s * D), BF16),
            pltpu.VMEM(wk.shape, BF16),
            pltpu.VMEM(wq.shape if first else qshape, BF16),
            pltpu.SemaphoreType.DMA((2,)),
        ],
        compiler_params=PARAMS,
        name="logits",
    )(*(far(xa, xb) if first else near(xa, xb)), *far(g, wk, wq if first else q))


def values_kernel(*refs):
    xs, (g, wv, out) = refs[:-3], refs[-3:]
    at = 0
    for x in xs:
        n, f = x.shape[1:]
        v = mm(norm(x[...].reshape(2 * n, f), g[...]), wv[...]).astype(BF16)
        for h in range(HEADS):
            out[h, at : at + n] = pair(v, n, h)
        at += n


def values(pieces, g, wv):
    s, _, f = pieces[0].shape
    total = sum(p.shape[1] for p in pieces)
    specs = [pl.BlockSpec((2, p.shape[1], f), lambda t: (t, 0, 0)) for p in pieces]
    return pl.pallas_call(
        values_kernel,
        grid=(s // 2,),
        in_specs=specs + [whole(g.shape), whole(wv.shape)],
        out_specs=pl.BlockSpec((HEADS, total, 2 * D), lambda t: (0, 0, t)),
        out_shape=pltpu.HBM((HEADS, total, s * D), BF16),
        compiler_params=PARAMS,
        name="values",
    )(*far(*pieces, g, wv))


def mix_kernel(p, v_h, x_h, wo_h, out, ms, v, x, wo, sems):
    pairs = HEADS // 2
    s = x.shape[0]
    copies = [
        pltpu.make_async_copy(v_h.at[2 * t : 2 * t + 2], v.at[2 * t : 2 * t + 2], sems.at[t]) for t in range(pairs)
    ]
    copies += [pltpu.make_async_copy(x_h, x, sems.at[pairs]), pltpu.make_async_copy(wo_h, wo, sems.at[pairs + 1])]
    for c in copies:
        c.start()
    for t in range(pairs):
        copies[t].wait()
        o = [mm(p[2 * t + h], v[2 * t + h]).astype(BF16) for h in range(2)]
        for r in range(s):
            ms[r, :, t * 2 * D : (t + 1) * 2 * D] = jnp.concatenate([head(o[0], r), head(o[1], r)], axis=1)
    copies[pairs].wait()
    copies[pairs + 1].wait()
    y = mm(ms[...].reshape(-1, x.shape[2]), wo[...])
    out[...] = (x[...].astype(F32) + y.reshape(x.shape)).astype(BF16)


def mix(p, v, x, wo):
    s, n, f = x.shape
    here = pl.BlockSpec(memory_space=pltpu.VMEM)
    there = pl.BlockSpec(memory_space=pl.ANY)
    return pl.pallas_call(
        mix_kernel,
        in_specs=[here, there, there, there],
        out_specs=here,
        out_shape=jax.ShapeDtypeStruct(x.shape, BF16),
        scratch_shapes=[
            pltpu.VMEM((s, n, f), BF16),
            pltpu.VMEM(v.shape, BF16),
            pltpu.VMEM((s, n, f), BF16),
            pltpu.VMEM(wo.shape, BF16),
            pltpu.SemaphoreType.DMA((HEADS // 2 + 2,)),
        ],
        compiler_params=PARAMS,
        name="mix",
    )(*near(p), *far(v, x, wo))


def column_kernel(h_ref, g, *refs):
    away, (out, xs, ns, qs, ks, vs, ms, w, sems) = refs[:4], refs[4:]
    copies = [pltpu.make_async_copy(z, w.at[i], sems.at[i]) for i, z in enumerate(away)]
    for c in copies:
        c.start()
    src, rows, f = h_ref.shape
    a = src * 8
    for i in range(0, rows, 16):
        y = h_ref[:, i : i + 16].astype(F32)
        for j in range(2):
            xs[pl.ds((i // 8 + j) * a, a)] = y[:, 8 * j : 8 * j + 8].reshape(a, f)

    def normed(p, carry):
        r = pl.ds(pl.multiple_of(p * a, a), a)
        ns[r] = norm(xs[r], g[...])
        return carry

    def attend(p, carry):
        r = pl.ds(pl.multiple_of(p * a, a), a)
        low = lax.broadcasted_iota(jnp.int32, (a, 2 * D), 1) < D
        zero = jnp.zeros((a, 2 * D), BF16)
        one = jnp.ones((a, 2 * D), BF16)
        ones = jnp.concatenate([jnp.where(low, one, zero), jnp.where(low, zero, one)], axis=0)
        for hp in range(HEADS // 2):
            c = slice(hp * 2 * D, (hp + 1) * 2 * D)
            q, k, v = qs[r, c], ks[r, c], vs[r, c]
            k = jnp.concatenate([jnp.where(low, k, zero), jnp.where(low, zero, k)], axis=0)
            v = jnp.concatenate([jnp.where(low, v, zero), jnp.where(low, zero, v)], axis=0)
            l = mm_t(q, k)
            e = []
            for z in (l[:, :a], l[:, a:]):
                e.append(jnp.exp2(z - jnp.max(z, axis=-1, keepdims=True)).astype(BF16))
            w = mm(jnp.concatenate(e, axis=1), jnp.concatenate([v, ones], axis=1))
            d = w[:, 2 * D :]
            i = pl.reciprocal(d, approx=True)
            ms[r, c] = (w[:, : 2 * D] * (i * (2.0 - d * i))).astype(BF16)
        return carry

    for p in range(rows // 8):
        r = slice(p * a, (p + 1) * a)
        n = norm(xs[r], g[...])
        if p == 0:
            copies[0].wait()
        qs[r] = (mm(n, w[0]) * (1.0 / (math.sqrt(D) * math.log(2.0)))).astype(BF16)
        if p == 0:
            copies[1].wait()
        ks[r] = mm(n, w[1]).astype(BF16)
        if p == 0:
            copies[2].wait()
        vs[r] = mm(n, w[2]).astype(BF16)
    lax.fori_loop(0, rows // 8, attend, 0, unroll=2)
    copies[3].wait()
    xs[...] = xs[...] + mm(ms[...], w[3])
    for i in range(0, rows, 16):
        y = [xs[pl.ds((i // 8 + j) * a, a)].reshape(src, 8, f) for j in range(2)]
        out[:, i : i + 16] = jnp.concatenate(y, axis=1).astype(BF16)


def column(hc, g, wq, wk, wv, wo):
    src, rows, f = hc.shape
    m = src * rows
    return pl.pallas_call(
        column_kernel,
        in_specs=[pl.BlockSpec(memory_space=pltpu.VMEM)] * 2 + [pl.BlockSpec(memory_space=pl.ANY)] * 4,
        out_specs=pl.BlockSpec(memory_space=pltpu.VMEM),
        out_shape=jax.ShapeDtypeStruct(hc.shape, BF16),
        scratch_shapes=[pltpu.VMEM((m, f), F32)]
        + [pltpu.VMEM((m, f), BF16)] * 5
        + [pltpu.VMEM((4, f, f), BF16), pltpu.SemaphoreType.DMA((4,))],
        compiler_params=PARAMS,
        name="column",
    )(*near(hc), *far(g, wq, wk, wv, wo))


def a2a(x):
    return lax.all_to_all(x, "seq", split_axis=0, concat_axis=0, tiled=True)


def shards(x, hg, wq, wk, wv, wo, vg, cq, ck, cv, co):
    S, N, F = x.shape
    hg = hg.reshape(1, F)
    vg = vg.reshape(1, F)
    barrier = lax.optimization_barrier

    def reduce(l):
        return a2a(l.reshape(SEQ, HEADS * N // SEQ, l.shape[-1]))

    xh = lax.ppermute(x, "res", XHI_SWAP)
    sib = lax.ppermute(x, "res", CORE_SWAP)

    def reduce_yz(l):
        half = SEQ // 2
        l = l.reshape(2, half, HEADS * N // SEQ, l.shape[-1]).transpose(1, 0, 2, 3)
        groups = [list(range(half)), list(range(half, SEQ))]
        l = lax.all_to_all(l, "seq", split_axis=0, concat_axis=0, tiled=True, axis_index_groups=groups)
        l = jnp.sum(l.astype(F32), axis=0)
        me = lax.axis_index("seq") // half
        other = lax.dynamic_index_in_dim(l, 1 - me, 0, keepdims=False).astype(BF16)
        mine = lax.dynamic_index_in_dim(l, me, 0, keepdims=False)
        return mine, lax.ppermute(other, "seq", [(i, (i + half) % SEQ) for i in range(SEQ)])

    q, l1 = logits(x, sib, hg, wk, wq=wq)
    r1 = reduce_yz(l1)
    xh, mine = barrier((xh, r1[0]))
    xhs = lax.ppermute(xh, "res", CORE_SWAP)
    (l2,) = logits(xh, xhs, hg, wk, q=q)
    odd = lax.axis_index("res") % 2 == 1
    early = lax.cond(
        odd, lambda l: values((x, sib, xh, xhs), hg, wv)[0, 0, 0] + l * 0, lambda l: jnp.zeros_like(l), l2[0, 0, 0]
    )
    l2, early = barrier((l2, early))
    r2 = jnp.sum(reduce(l2).astype(F32), axis=0)
    x_late, l2 = barrier((x, l2))
    v = values((x_late, sib, xh, xhs), hg, wv)
    scale = 1.0 / (math.sqrt(D) * math.sqrt(S * SEQ))
    tied = jnp.concatenate([mine + r1[1].astype(F32), r2 + early.astype(F32) * 0], axis=-1) * scale
    probs = jax.nn.softmax(tied, axis=-1).astype(BF16)
    probs = a2a(jnp.broadcast_to(probs[None], (SEQ,) + probs.shape)).reshape(HEADS, N, 4 * N)
    hid = mix(probs, v, x, wo)
    G = N // SEQ
    t = jnp.transpose(hid.reshape(S, SEQ, G, F), (1, 2, 0, 3)).reshape(SEQ, G * S, F)
    o = a2a(column(a2a(t), vg, cq, ck, cv, co))
    return jnp.transpose(o.reshape(SEQ, G, S, F), (2, 0, 1, 3)).reshape(S, N, F)


def solution(mesh):
    in_specs = (P("seq", "res", None),) + (P(),) * 10
    return jax.shard_map(shards, mesh=mesh, in_specs=in_specs, out_specs=P("seq", "res", None), check_vma=False)
```
